32 devices in a mesh: kp: 8 (over z, x), kz: 4 (over y, core).
Axes of the slice: x: 2, y: 2, z: 4, core: 2. Of those that a mesh axis runs over, the one named last changes fastest.
Arguments:
- orbitals: bfloat16 [8, 4, 2, 64, 1024], P('kp', 'kz'), may hold values from -0.75 to 0.75
- trial_vectors: bfloat16 [8, 4, 2, 2, 1024], P('kp', 'kz'), may hold values from -6 to 6
- screened_table: bfloat16 [64, 2, 1024, 1024], P('kp', None, 'kz'), may hold values from -0.09375 to 0.09375
- shift_inplane: int32 [2], replicated, may hold values from -32 to 31
- shift_depth: int32 [2], replicated, may hold values from -16 to 15
- table_entry: int32 [2], replicated, may hold values from 0 to 63
Outputs:
- kernel_image: float32 [8, 4, 2, 2, 1024], P('kp', 'kz')
The draws below stay inside these ranges and needn't reach their ends.
All inputs are finite; a program needn't handle non-finite values.
Results may differ from the reference program's by a relative error of at most 0.0049.
Values may be sent and summed in bfloat16 or wider, within the bound.
No kernel may reach another device: no remote copies, remote signals or barrier semaphores. Data moves between devices by JAX's collectives and lax.ppermute only.
A program may use at most 64 MiB of HBM per device.

```python
import jax
import jax.numpy as jnp
from jax import lax

NMU = 1024
NV = 32
NC = 32
NTV = 2
NB = 64
KP = 8
KZ = 4
NWQ = 64


def steps_of(own_key, shape, pieces, smallest, high):
    def one(position, blocks):
        steps = jax.random.uniform(jax.random.fold_in(jax.random.fold_in(own_key, 6), position), (blocks,), jnp.float32, smallest / len(pieces), high / len(pieces))
        return jnp.repeat(jnp.exp(steps), shape[position] // blocks).reshape((-1,) + (1,) * (len(shape) - position - 1))

    level = one(*pieces[0])
    for cut in pieces[1:]:
        level = level * one(*cut)
    return level


def centred(key, shape, spread, reach, shards=(), kind=jnp.bfloat16):
    gain = steps_of(key, shape, shards, -0.22, 0.18) if shards else 1.0
    values = jax.random.normal(key, shape, jnp.float32) * spread * gain
    return jnp.minimum(jnp.maximum(values, -reach), reach).astype(kind)


def setup_inputs(seed: int = 0) -> dict:
    seeds = jax.random.split(jax.random.key(seed), 7)
    return {
        "orbitals": centred(seeds[0], (KP, KZ, 2, NB, NMU), 0.125, 0.75, ((0, 8), (1, 4))),
        "trial_vectors": centred(seeds[1], (KP, KZ, NTV, 2, NC * NV), 1.0, 6.0, ((0, 8), (1, 4))),
        "screened_table": centred(seeds[2], (NWQ, 2, NMU, NMU), 0.015625, 0.09375, ((0, 8), (2, 4))),
        "shift_inplane": jax.random.randint(seeds[3], (2,), -4 * KP, 4 * KP).astype(jnp.int32),
        "shift_depth": jax.random.randint(seeds[4], (2,), -4 * KZ, 4 * KZ).astype(jnp.int32),
        "table_entry": jax.random.randint(seeds[5], (2,), 0, NWQ).astype(jnp.int32),
    }


def pair_term(own_valence, own_conduction, next_valence, next_conduction, next_trial, screen_rows):
    valence_count = own_valence.shape[1]
    conduction_count = own_conduction.shape[1]
    row_span = own_conduction.shape[2]
    points = own_valence.shape[2]
    vector_count = next_trial.shape[0]
    trial_matrix = next_trial.reshape(vector_count, 2, conduction_count, valence_count)
    real_part = jnp.swapaxes(trial_matrix[:, 0], 1, 2)
    imag_part = jnp.swapaxes(trial_matrix[:, 1], 1, 2)
    upper_rows = jnp.concatenate([real_part, -imag_part], axis=2)
    lower_rows = jnp.concatenate([imag_part, real_part], axis=2)
    coeffs = jnp.stack([upper_rows, lower_rows], axis=1).reshape(vector_count * 2 * valence_count, 2 * conduction_count)
    amplitude = jnp.dot(coeffs, next_conduction.reshape(2 * conduction_count, row_span), preferred_element_type=jnp.float32)
    amplitude = amplitude.astype(jnp.bfloat16).reshape(vector_count, 2, valence_count, row_span)
    partner_rows = next_valence.reshape(2 * valence_count, points)
    own_real = own_valence[0]
    own_imag = own_valence[1]
    valence_stack = jnp.concatenate([jnp.concatenate([own_real, -own_imag], axis=1), jnp.concatenate([own_imag, own_real], axis=1)], axis=0)
    block = min(512, row_span)

    def one_vector(amplitude_pair):
        amp_real = amplitude_pair[0]
        amp_imag = amplitude_pair[1]

        def add_block(block_index, accumulated):
            row_start = block_index * block
            part_real = lax.dynamic_slice_in_dim(amp_real, row_start, block, 1)
            part_imag = lax.dynamic_slice_in_dim(amp_imag, row_start, block, 1)
            left_factor = jnp.concatenate([jnp.concatenate([part_real, part_imag], axis=0), jnp.concatenate([part_imag, -part_real], axis=0)], axis=1)
            expanded = lax.dot_general(left_factor, partner_rows, (((0,), (0,)), ((), ())), preferred_element_type=jnp.float32)
            exp_real = expanded[:block]
            exp_imag = expanded[block:]
            screen_part = lax.dynamic_slice_in_dim(screen_rows, row_start, block, 1)
            w_real = screen_part[0].astype(jnp.float32)
            w_imag = screen_part[1].astype(jnp.float32)
            product = jnp.concatenate([w_real * exp_real - w_imag * exp_imag, w_real * exp_imag + w_imag * exp_real], axis=1).astype(jnp.bfloat16)
            half_product = lax.dot_general(product, valence_stack, (((1,), (1,)), ((), ())), preferred_element_type=jnp.float32).astype(jnp.bfloat16)
            half_real = half_product[:, :valence_count]
            half_imag = half_product[:, valence_count:]
            half_stack = jnp.concatenate([jnp.concatenate([half_real, half_imag], axis=1), jnp.concatenate([half_imag, -half_real], axis=1)], axis=0)
            cond_part = lax.dynamic_slice_in_dim(own_conduction, row_start, block, 2)
            cond_cat = jnp.concatenate([cond_part[0], cond_part[1]], axis=1)
            return accumulated + jnp.dot(cond_cat, half_stack, preferred_element_type=jnp.float32)

        result = lax.fori_loop(0, row_span // block, add_block, jnp.zeros((conduction_count, 2 * valence_count), jnp.float32))
        return jnp.stack([result[:, :valence_count].reshape(-1), result[:, valence_count:].reshape(-1)])

    return lax.map(one_vector, amplitude)


def reference(orbitals, trial_vectors, screened_table, shift_inplane, shift_depth, table_entry):
    plane_count = orbitals.shape[0]
    depth_count = orbitals.shape[1]

    def one_point(flat_index):
        plane_index = flat_index // depth_count
        depth_index = flat_index % depth_count
        own_orbitals = orbitals[plane_index, depth_index]
        accumulated = jnp.zeros(trial_vectors.shape[2:], jnp.float32)
        for transfer in range(2):
            plane_next = ((plane_index + shift_inplane[transfer]) % plane_count).astype(jnp.int32)
            depth_next = ((depth_index + shift_depth[transfer]) % depth_count).astype(jnp.int32)
            partner = orbitals[plane_next, depth_next]
            partner_trial = trial_vectors[plane_next, depth_next]
            screen_full = screened_table[table_entry[transfer]]
            accumulated = accumulated + pair_term(own_orbitals[:, :NV], own_orbitals[:, NV:], partner[:, :NV], partner[:, NV:], partner_trial, screen_full)
        return accumulated

    result = lax.map(one_point, jnp.arange(plane_count * depth_count, dtype=jnp.int32))
    return result.reshape(trial_vectors.shape)
```

```python
import functools

import jax
import jax.numpy as jnp
from jax import lax
from jax.experimental import pallas as pl
from jax.experimental.pallas import tpu as pltpu
from jax.sharding import PartitionSpec as P

NV = 32
PAIR = 2
F32 = jnp.float32
BF16 = jnp.bfloat16


def swapped(block, axis):
    return lax.ppermute(block, axis, [(i, i ^ 1) for i in range(lax.axis_size(axis))])


def passed_along(block, distance):
    size = lax.axis_size("kp")
    return lax.ppermute(block, "kp", [(i, (i + PAIR * distance) % size) for i in range(size)])


def packed(orbitals, trial_vectors, planes, depths):
    bands = orbitals.shape[1]
    points = orbitals.shape[2]
    vectors = trial_vectors.shape[0]
    conduction = bands - NV
    half = points // (planes * PAIR)
    rows = points // (depths * PAIR * PAIR)
    valence = orbitals[:, :NV].reshape(2 * NV, planes, 1, 1, PAIR, half)
    valence = valence.transpose(1, 2, 3, 4, 0, 5)
    cond = orbitals[:, NV:].reshape(2 * conduction, 1, depths, PAIR, PAIR, rows)
    cond = cond.transpose(1, 4, 2, 3, 0, 5)
    trial = trial_vectors.reshape(vectors, 2, conduction, NV).transpose(2, 0, 1, 3)
    width = vectors * 2 * NV
    trial = trial.reshape(conduction, width)
    lead = (planes, PAIR, depths, PAIR)
    parts = [
        jnp.broadcast_to(valence, lead + valence.shape[4:]),
        jnp.broadcast_to(cond, lead + cond.shape[4:]),
    ]
    trial = trial.reshape(1, 1, 1, PAIR, conduction // PAIR, width)
    trial = jnp.broadcast_to(trial, lead + trial.shape[4:])
    count = planes * PAIR * depths * PAIR
    if half == rows == width:
        return (jnp.concatenate(parts + [trial], axis=4).reshape(count, -1, half),)
    return tuple(part.reshape((count,) + part.shape[4:]) for part in parts + [trial])


def screen_blocks(table, table_entry, lanes, planes, depths):
    slots, _, span, points = table.shape
    plane = lax.axis_index("kp") // PAIR
    side = lax.axis_index("kp") % PAIR
    core = lax.axis_index("kz") % PAIR
    rows = span // PAIR
    columns = points // planes
    half = columns // PAIR
    owner = table_entry // slots
    slot = table_entry % slots
    owner_plane = owner // PAIR
    owner_side = owner % PAIR
    mine = lax.axis_index("kp")
    if lanes == 1:
        first = plane == owner_plane[0]
        choices = [
            (
                jnp.where(mine == owner[0], slot[0], slot[1]),
                jnp.where(first, owner_side[0], owner_side[1]),
            )
        ]
    else:
        choices = [(slot[t], owner_side[t]) for t in range(2)]

    def cut(which, part):
        return lax.dynamic_slice(table, (which, 0, part * rows, 0), (1, 2, rows, points))[0]

    held = []
    for which, source_side in choices:
        arrived = swapped(cut(which, 1 - side), "kp")
        held.append(jnp.where(source_side == side, cut(which, side), arrived))
    held = jnp.stack(held)

    def columns_of(target):
        start = target * columns
        near = lax.dynamic_slice_in_dim(held, start + core * half, half, 3)
        far = lax.dynamic_slice_in_dim(held, start + (1 - core) * half, half, 3)
        return jnp.concatenate([near, far], axis=3)

    blocks = [columns_of(plane)]
    for distance in range(1, planes):
        blocks.append(passed_along(columns_of((plane + distance) % planes), distance))
    blocks = jnp.stack(blocks)
    picked = []
    for t in range(2):
        distance = (plane - owner_plane[t]) % planes
        lane = 0 if lanes == 1 else t
        picked.append(lax.dynamic_index_in_dim(blocks, distance, 0, keepdims=False)[lane])
    return jnp.stack(picked)


def compute(
    core_ref, own_ref, near_ref, far_ref, cond_ref, tri_near_ref, tri_far_ref, screen_ref,
    out_ref, wide_ref, sums_ref,
):
    count, pair_bands, rows = cond_ref.shape
    conduction = pair_bands // 2
    width = out_ref.shape[2]
    vectors = width // (2 * NV)
    wide_ref[...] = screen_ref[...].astype(F32)
    sums_ref[...] = jnp.zeros_like(sums_ref)
    lane = lax.broadcasted_iota(jnp.int32, (conduction, width), 1)
    low = lane % (2 * NV) < NV
    vector_of = lane // (2 * NV)
    core = core_ref[0]

    def turned(x):
        return jnp.where(low, -pltpu.roll(x, width - NV, 1), pltpu.roll(x, NV, 1))

    def valence_of(k):
        return jnp.concatenate([near_ref[k], far_ref[k]], axis=1)

    def step(partner, carry):
        valence = valence_of(partner)
        near = tri_near_ref[partner].astype(F32)
        far = tri_far_ref[partner].astype(F32)
        trial = jnp.concatenate(
            [jnp.where(core == 0, near, far), jnp.where(core == 0, far, near)], axis=0
        )
        turn = turned(trial)
        coeffs = jnp.concatenate(
            [
                jnp.concatenate([trial, -turn], axis=1),
                jnp.concatenate([turn, trial], axis=1),
            ],
            axis=0,
        ).astype(BF16)
        amplitude = lax.dot_general(
            cond_ref[partner], coeffs, (((0,), (0,)), ((), ())), preferred_element_type=F32
        ).astype(BF16)
        left = jnp.concatenate([amplitude[:, :width], amplitude[:, width:]], axis=0)
        screened = [[], []]
        blank = jnp.zeros_like(valence)
        for n in range(vectors):
            right = jnp.concatenate([valence if m == n else blank for m in range(vectors)], axis=0)
            expanded = jnp.dot(left, right, preferred_element_type=F32)
            real = expanded[:rows]
            imag = expanded[rows:]
            for t in range(2):
                w_real = wide_ref[t, 0]
                w_imag = wide_ref[t, 1]
                screened[t].append(
                    (
                        (w_real * real - w_imag * imag).astype(BF16),
                        (w_real * imag + w_imag * real).astype(BF16),
                    )
                )
        for t in range(2):
            own = own_ref[t, partner]
            mine = valence_of(own)
            cross = jnp.concatenate([-mine[NV:], mine[:NV]], axis=0)
            copies = [mine] * vectors
            crosses = [cross] * vectors
            s_real = jnp.concatenate([s[0] for s in screened[t]], axis=0)
            s_imag = jnp.concatenate([s[1] for s in screened[t]], axis=0)
            contract = (((1,), (1,)), ((), ()))
            half = lax.dot_general(
                s_real, jnp.concatenate(copies, axis=0), contract, preferred_element_type=F32
            ) + lax.dot_general(
                s_imag, jnp.concatenate(crosses, axis=0), contract, preferred_element_type=F32
            )
            half = half.astype(BF16)
            upper = jnp.zeros((conduction, width), F32)
            lower = jnp.zeros((conduction, width), F32)
            for n in range(vectors):
                product = jnp.dot(
                    cond_ref[own], half[n * rows : (n + 1) * rows], preferred_element_type=F32
                )
                upper = jnp.where(vector_of == n, product[:conduction], upper)
                lower = jnp.where(vector_of == n, product[conduction:], lower)
            sums_ref[own] += upper - turned(lower)
        return carry

    lax.fori_loop(0, count, step, 0)
    out_ref[...] = sums_ref[...].astype(BF16)


def shards(orbitals, trial_vectors, screened_table, shift_inplane, shift_depth, table_entry):
    plane_size = lax.axis_size("kp")
    depth_size = lax.axis_size("kz")
    planes = plane_size // PAIR
    depths = depth_size // PAIR
    count = plane_size * depth_size
    vectors = trial_vectors.shape[2]
    conduction = orbitals.shape[3] - NV
    axes = ("kp", "kz")
    own_orbitals = orbitals[0, 0]
    own_trial = trial_vectors[0, 0]
    ids = jnp.arange(count, dtype=jnp.int32)
    own = jnp.stack(
        [
            (ids // depth_size - shift_inplane[t]) % plane_size * depth_size
            + (ids % depth_size - shift_depth[t]) % depth_size
            for t in range(2)
        ]
    ).astype(jnp.int32)
    core = (lax.axis_index("kz") % PAIR).astype(jnp.int32).reshape(1)

    def run(lanes):
        sent = packed(own_orbitals, own_trial, planes, depths)
        came = [lax.all_to_all(part, axes, 0, 0, tiled=True) for part in sent]
        if len(came) == 1:
            both = came[0]
            near = both[:, : 2 * NV]
            cond = both[:, 2 * NV : 2 * (NV + conduction)]
            tri_near = both[:, 2 * (NV + conduction) :]
        else:
            near, cond, tri_near = came
        far, tri_far = swapped((near, tri_near), "kz")
        screen = screen_blocks(screened_table, table_entry, lanes, planes, depths)
        width = vectors * 2 * NV
        vmem = pl.BlockSpec(memory_space=pltpu.VMEM)
        smem = pl.BlockSpec(memory_space=pltpu.SMEM)
        partial = pl.pallas_call(
            compute,
            out_shape=jax.ShapeDtypeStruct((count, conduction, width), BF16),
            in_specs=[smem, smem] + [vmem] * 6,
            out_specs=vmem,
            scratch_shapes=[
                pltpu.VMEM(screen.shape, F32),
                pltpu.VMEM((count, conduction, width), F32),
            ],
            compiler_params=pltpu.CompilerParams(vmem_limit_bytes=56 << 20),
        )(core, own, near, far, cond, tri_near, tri_far, screen)
        terms = lax.all_to_all(partial, axes, 0, 0, tiled=True)
        image = jnp.sum(terms.astype(F32), axis=0)
        image = image.reshape(conduction, vectors, 2, NV).transpose(1, 2, 0, 3)
        return image.reshape(1, 1, vectors, 2, conduction * NV)

    owner_plane = table_entry // screened_table.shape[0] // PAIR
    return lax.cond(
        owner_plane[0] == owner_plane[1],
        functools.partial(run, 2),
        functools.partial(run, 1),
    )


def solution(mesh):
    in_specs = (
        P("kp", "kz", None, None, None),
        P("kp", "kz", None, None, None),
        P("kp", None, "kz", None),
        P(),
        P(),
        P(),
    )
    out_specs = P("kp", "kz", None, None, None)
    return jax.shard_map(shards, mesh=mesh, in_specs=in_specs, out_specs=out_specs, check_vma=False)
```

```python
import functools
import math

import jax
import jax.numpy as jnp
from jax import lax
from jax.experimental import pallas as pl
from jax.experimental.pallas import tpu as pltpu
from jax.sharding import PartitionSpec as P

NV = 32
PAIR = 2
GROUP = 8
F32 = jnp.float32
BF16 = jnp.bfloat16


def swapped(block, axis):
    return lax.ppermute(block, axis, [(i, i ^ 1) for i in range(lax.axis_size(axis))])


def passed_along(block, distance):
    size = lax.axis_size("kp")
    return lax.ppermute(block, "kp", [(i, (i + PAIR * distance) % size) for i in range(size)])


def packed(orbitals, trial_vectors, planes, depths):
    bands = orbitals.shape[1]
    points = orbitals.shape[2]
    vectors = trial_vectors.shape[0]
    conduction = bands - NV
    half = points // (planes * PAIR)
    rows = points // (depths * PAIR * PAIR)
    width = vectors * 2 * conduction
    valence = orbitals[:, :NV].reshape(2 * NV, planes, 1, 1, PAIR, half)
    valence = valence.transpose(1, 2, 3, 4, 0, 5)
    cond = orbitals[:, NV:].reshape(2 * conduction, 1, depths, PAIR, PAIR, rows)
    cond = cond.transpose(1, 4, 2, 3, 0, 5)
    trial = trial_vectors.reshape(vectors, 2, conduction, NV).transpose(3, 0, 1, 2)
    trial = trial.reshape(1, 1, 1, PAIR, NV // PAIR, width)
    lead = (planes, PAIR, depths, PAIR)
    parts = [jnp.broadcast_to(part, lead + part.shape[4:]) for part in (valence, trial, cond)]
    count = planes * PAIR * depths * PAIR
    if half == rows == width:
        return (jnp.concatenate(parts, axis=4).reshape(count, -1, half),)
    return tuple(part.reshape((count,) + part.shape[4:]) for part in parts)


def screen_lanes(table, owner, slot, lanes):
    rows = table.shape[2] // PAIR
    points = table.shape[3]
    mine = lax.axis_index("kp")
    side = lax.rem(mine, PAIR)
    if lanes == 1:
        choices = [jnp.where(mine == owner[0], slot[0], slot[1])]
    else:
        choices = slot

    def cut(which, part):
        return lax.dynamic_slice(table, (which, 0, part * rows, 0), (1, 2, rows, points))

    leaving = jnp.concatenate([cut(which, 1 - side) for which in choices], axis=0)
    staying = jnp.concatenate([cut(which, side) for which in choices], axis=0)
    return leaving, staying


def screen_blocks(staying, arrived, owner, lanes, planes):
    points = staying.shape[3]
    mine = lax.axis_index("kp")
    plane = lax.div(mine, PAIR)
    side = lax.rem(mine, PAIR)
    core = lax.rem(lax.axis_index("kz"), PAIR)
    columns = points // planes
    half = columns // PAIR
    owner_plane = [lax.div(o, PAIR) for o in owner]
    owner_side = [lax.rem(o, PAIR) for o in owner]
    if lanes == 1:
        sources = [jnp.where(plane == owner_plane[0], owner_side[0], owner_side[1])]
    else:
        sources = owner_side
    held = jnp.concatenate(
        [jnp.where(s == side, staying[i : i + 1], arrived[i : i + 1]) for i, s in enumerate(sources)]
    )

    def columns_of(target):
        start = target * columns
        near = lax.dynamic_slice_in_dim(held, start + core * half, half, 3)
        far = lax.dynamic_slice_in_dim(held, start + (1 - core) * half, half, 3)
        return jnp.concatenate([near, far], axis=3)

    blocks = [columns_of(plane)]
    for distance in range(1, planes):
        blocks.append(passed_along(columns_of(lax.rem(plane + distance, planes)), distance))
    blocks = jnp.stack(blocks)
    picked = []
    for t in range(2):
        distance = lax.rem(plane - owner_plane[t] + planes, planes)
        lane = 0 if lanes == 1 else t
        picked.append(lax.dynamic_index_in_dim(blocks, distance, 0, keepdims=False)[lane])
    return jnp.stack(picked)


def compute(sizes, inplane_ref, depth_ref, *refs):
    plane_size, depth_size, conduction, pieces = sizes
    came = refs[: 2 * pieces - 1 if pieces > 1 else 2]
    screen_ref, out_ref, wide_ref, left_ref, screened_ref, half_ref = refs[len(came) :]
    count, _, width = out_ref.shape
    rows = wide_ref.shape[3]
    columns = wide_ref.shape[2]
    group = 2 * conduction
    vectors = width // group
    span = vectors * rows
    share = NV // PAIR
    if pieces == 1:
        here, there = came
        near = lambda k: here[k, : 2 * NV]
        far = lambda k: there[k, : 2 * NV]
        trial_near = lambda k: here[k, 2 * NV : 2 * NV + share]
        trial_far = lambda k: there[k, 2 * NV : 2 * NV + share]
        cond_of = lambda k: here[k, 2 * NV + share :]
    else:
        near, trial_near, cond_of, far, trial_far = [
            functools.partial(lambda ref, k: ref[k], ref) for ref in came
        ]
    lane = lax.broadcasted_iota(jnp.int32, (NV, width), 1)
    low = lane % group < conduction
    vector_of = lane // group
    core = lax.rem(lax.axis_index("kz"), PAIR)
    moves = [
        (
            lax.rem(lax.rem(inplane_ref[t], plane_size) + plane_size, plane_size),
            lax.rem(lax.rem(depth_ref[t], depth_size) + depth_size, depth_size),
        )
        for t in range(2)
    ]

    def own_of(partner, t):
        plane = lax.rem(lax.div(partner, depth_size) + plane_size - moves[t][0], plane_size)
        depth = lax.rem(lax.rem(partner, depth_size) + depth_size - moves[t][1], depth_size)
        return plane * depth_size + depth

    def exchanged(x):
        return jnp.where(
            low, pltpu.roll(x, width - conduction, 1), pltpu.roll(x, conduction, 1)
        )

    def valence_of(k):
        return jnp.concatenate([near(k), far(k)], axis=1)

    def amplitude(k, spot):
        first = trial_near(k).astype(F32)
        second = trial_far(k).astype(F32)
        trial = jnp.concatenate(
            [jnp.where(core == 0, first, second), jnp.where(core == 0, second, first)], axis=0
        )
        cross = exchanged(trial)
        trial = jnp.where(low, trial, -trial)
        coeffs = []
        for n in range(vectors):
            a = trial if n == 0 else pltpu.roll(trial, width - n * group, 1)
            b = cross if n == 0 else pltpu.roll(cross, width - n * group, 1)
            coeffs += [a, b, b, -a]
        coeffs = jnp.concatenate(coeffs, axis=0)[:, :group].astype(BF16)
        left_ref[spot] = jnp.dot(coeffs, cond_of(k), preferred_element_type=F32).astype(BF16)

    def expand(partner, spot):
        left = left_ref[spot]
        left = jnp.concatenate(
            [left[2 * NV * i : 2 * NV * (i + 1)] for i in range(2 * vectors)], axis=1
        )
        expanded = lax.dot_general(
            valence_of(partner), left, (((0,), (0,)), ((), ())), preferred_element_type=F32
        )
        for t in range(2):
            own = own_of(partner, t)
            w_real = wide_ref[t, 0]
            w_imag = wide_ref[t, 1]
            for n in range(vectors):
                real = expanded[:, 2 * n * rows : (2 * n + 1) * rows]
                imag = expanded[:, (2 * n + 1) * rows : (2 * n + 2) * rows]
                at = pl.ds((t * vectors + n) * rows, rows)
                screened_ref[own, :columns, at] = (w_real * real - w_imag * imag).astype(BF16)
                screened_ref[own, columns:, at] = (w_real * imag + w_imag * real).astype(BF16)

    def halve(k, spot):
        valence = valence_of(k)
        cross = jnp.concatenate([-valence[NV:], valence[:NV]], axis=0)
        both = jnp.dot(
            jnp.concatenate([valence, cross], axis=1), screened_ref[k], preferred_element_type=F32
        )
        half_ref[spot] = (both[:, :span] + both[:, span:]).astype(BF16)

    def finish(k, spot):
        half = half_ref[spot]
        cond = cond_of(k)
        cond = jnp.concatenate([cond] * vectors, axis=0)
        image = jnp.zeros((NV, width), F32)
        for n in range(vectors):
            product = lax.dot_general(
                half[:, n * rows : (n + 1) * rows],
                cond,
                (((1,), (1,)), ((), ())),
                preferred_element_type=F32,
            )
            real = product[:NV]
            imag = product[NV:]
            term = exchanged(imag) + jnp.where(low, real, -real)
            image = jnp.where(vector_of == n, term, image)
        out_ref[k] = image.astype(BF16)

    def in_groups(*steps):
        size = left_ref.shape[0]

        def group_of(index, carry):
            for step in steps:
                for spot in range(size):
                    step(index * size + spot, spot)
            return carry

        lax.fori_loop(0, count // size, group_of, 0)

    for t in range(2):
        for part in range(2):
            wide_ref[t, part] = screen_ref[t, part].astype(F32).T
    in_groups(amplitude, expand)
    in_groups(halve, finish)


def shards(orbitals, trial_vectors, screened_table, shift_inplane, shift_depth, table_entry):
    plane_size = lax.axis_size("kp")
    depth_size = lax.axis_size("kz")
    planes = plane_size // PAIR
    depths = depth_size // PAIR
    count = plane_size * depth_size
    vectors = trial_vectors.shape[2]
    conduction = orbitals.shape[3] - NV
    points = orbitals.shape[4]
    width = vectors * 2 * conduction
    axes = ("kp", "kz")
    slots = screened_table.shape[0]
    entry = [table_entry[t] for t in range(2)]
    owner = [lax.div(e, slots) for e in entry]
    slot = [lax.rem(e, slots) for e in entry]

    def run(lanes):
        leaving, staying = screen_lanes(screened_table, owner, slot, lanes)
        leaving, own_orbitals, own_trial = lax.optimization_barrier(
            (leaving, orbitals[0, 0], trial_vectors[0, 0])
        )
        arrived = swapped(leaving, "kp")
        sent = packed(own_orbitals, own_trial, planes, depths)
        came = tuple(lax.all_to_all(part, axes, 0, 0, tiled=True) for part in sent)
        if len(came) == 1:
            there = (swapped(came[0][:, : 2 * NV + NV // PAIR], "kz"),)
        else:
            there = swapped(came[:2], "kz")
        screen = screen_blocks(staying, arrived, owner, lanes, planes)
        rows, columns = screen.shape[2:]
        batch = math.gcd(count, GROUP)
        operands = came + tuple(there) + (screen,)
        vmem = pl.BlockSpec(memory_space=pltpu.VMEM)
        smem = pl.BlockSpec(memory_space=pltpu.SMEM)
        partial = pl.pallas_call(
            functools.partial(compute, (plane_size, depth_size, conduction, len(came))),
            out_shape=jax.ShapeDtypeStruct((count, NV, width), BF16),
            in_specs=[smem, smem] + [vmem] * len(operands),
            out_specs=vmem,
            scratch_shapes=[
                pltpu.VMEM((2, 2, columns, rows), F32),
                pltpu.VMEM((batch, vectors * 4 * NV, rows), BF16),
                pltpu.VMEM((count, 2 * columns, 2 * vectors * rows), BF16),
                pltpu.VMEM((batch, 2 * NV, vectors * rows), BF16),
            ],
            compiler_params=pltpu.CompilerParams(vmem_limit_bytes=56 << 20),
        )(shift_inplane, shift_depth, *operands)
        terms = lax.all_to_all(partial, axes, 0, 0, tiled=True)
        image = jnp.sum(terms.astype(F32), axis=0)
        image = image.reshape(NV, vectors, 2, conduction).transpose(1, 2, 3, 0)
        return image.reshape(1, 1, vectors, 2, conduction * NV)

    return lax.cond(
        lax.div(owner[0], PAIR) == lax.div(owner[1], PAIR),
        functools.partial(run, 2),
        functools.partial(run, 1),
    )


def solution(mesh):
    in_specs = (
        P("kp", "kz", None, None, None),
        P("kp", "kz", None, None, None),
        P("kp", None, "kz", None),
        P(),
        P(),
        P(),
    )
    out_specs = P("kp", "kz", None, None, None)
    return jax.shard_map(shards, mesh=mesh, in_specs=in_specs, out_specs=out_specs, check_vma=False)
```

```python
import functools
import math

import jax
import jax.numpy as jnp
from jax import lax
from jax.experimental import pallas as pl
from jax.experimental.pallas import tpu as pltpu
from jax.sharding import PartitionSpec as P

NV = 32
PAIR = 2
GROUP = 8
F32 = jnp.float32
BF16 = jnp.bfloat16


def swapped(block, axis):
    return lax.ppermute(block, axis, [(i, i ^ 1) for i in range(lax.axis_size(axis))])


def passed_along(block, distance):
    size = lax.axis_size("kp")
    return lax.ppermute(block, "kp", [(i, (i + PAIR * distance) % size) for i in range(size)])


def neighbour(block, flip, distance):
    planes_sides = lax.axis_size("kp")
    size = lax.axis_size("kz")
    route = []
    for p in range(planes_sides):
        for k in range(size):
            to = (p ^ flip) * size + (k + PAIR * distance) % size
            route.append((p * size + k, to))
    return lax.ppermute(block, ("kp", "kz"), route)


def merged(columns, width):
    return columns % width == 0 and NV * width % columns == 0 and NV * width // columns % 16 == 0


def cut_orbitals(planes, orbitals_ref, trial_ref, cond_ref, *bundle_refs):
    points = orbitals_ref.shape[2]
    columns = points // planes
    count, _, rows = cond_ref.shape
    blocks = points // rows
    depths = blocks // PAIR // PAIR
    plane = lax.div(lax.axis_index("kp"), PAIR)
    cond = jnp.concatenate([orbitals_ref[0, NV:], orbitals_ref[1, NV:]], axis=0)
    for block in range(blocks):
        piece = cond[:, block * rows : (block + 1) * rows]
        side, depth_core = block % PAIR, block // PAIR
        for target in range(planes):
            cond_ref[(target * PAIR + side) * depths * PAIR + depth_core] = piece
    share = bundle_refs[0].shape[0] - 2 * NV
    width = trial_ref.shape[1]

    def fill(ref, at):
        for part in range(2):
            ref[part * NV : (part + 1) * NV] = orbitals_ref[part, :NV, at]

    for distance, ref in enumerate(bundle_refs):
        target = lax.rem(plane + distance, planes)
        if columns % 128 == 0:
            fill(ref, pl.ds(pl.multiple_of(target * columns, columns), columns))
        else:
            for spot in range(planes):
                at = slice(spot * columns, (spot + 1) * columns)
                pl.when(target == spot)(functools.partial(fill, ref, at))
        if share:
            for piece in range(columns // width):
                ref[2 * NV :, piece * width : (piece + 1) * width] = trial_ref[
                    piece * share : (piece + 1) * share
                ]


def packed(orbitals, trial_vectors, planes, depths):
    bands, points = orbitals.shape[1:]
    vectors = trial_vectors.shape[0]
    conduction = bands - NV
    columns = points // planes
    rows = points // (depths * PAIR * PAIR)
    count = planes * PAIR * depths * PAIR
    width = vectors * 2 * conduction
    trial = trial_vectors.reshape(vectors, 2, conduction, NV).transpose(3, 0, 1, 2)
    trial = trial.reshape(NV, width)
    share = NV * width // columns if merged(columns, width) else 0
    cond_shape = jax.ShapeDtypeStruct((count, 2 * conduction, rows), orbitals.dtype)
    bundle_shape = jax.ShapeDtypeStruct((2 * NV + share, columns), orbitals.dtype)
    vmem = pl.BlockSpec(memory_space=pltpu.VMEM)
    cond, *bundles = pl.pallas_call(
        functools.partial(cut_orbitals, planes),
        out_shape=(cond_shape,) + (bundle_shape,) * planes,
        in_specs=[vmem, vmem],
        out_specs=(vmem,) * (planes + 1),
        compiler_params=pltpu.CompilerParams(vmem_limit_bytes=32 << 20),
    )(orbitals, trial)
    parts = [bundles]
    if not share:
        parts.append([trial] * planes)
    return cond, parts


def collected(blocks):
    return jnp.stack(
        [passed_along(block, d) if d else block for d, block in enumerate(blocks)]
    )


def gathered(column, depths):
    here = [
        neighbour(column, flip, distance) if flip or distance else column
        for flip in range(PAIR)
        for distance in range(depths)
    ]
    return here


def cut_slabs(lanes, planes, entry_ref, table_ref, *refs):
    leaving, staying = refs[:planes], refs[planes : 2 * planes]
    slab_ref, sems = refs[2 * planes :]
    slots = table_ref.shape[0]
    points = table_ref.shape[3]
    rows, columns = leaving[0].shape[2:]
    direct = columns % 128 == 0
    mine = lax.axis_index("kp")
    plane = lax.div(mine, PAIR)
    side = lax.rem(mine, PAIR)
    for lane in range(lanes):
        entry = entry_ref[lane]
        if lanes == 1:
            entry = jnp.where(lax.div(entry, slots) == mine, entry, entry_ref[1])
        slot = lax.rem(entry, slots)
        owned = lax.div(entry, slots) == mine

        def bring():
            copies = []
            for spot, (part, outs) in enumerate(((1 - side, leaving), (side, staying))):
                within = pl.ds(pl.multiple_of(part * rows, rows), rows)
                if direct:
                    for distance, out_ref in enumerate(outs):
                        start = lax.rem(plane + distance, planes) * columns
                        at = pl.ds(pl.multiple_of(start, columns), columns)
                        copies.append(
                            pltpu.make_async_copy(
                                table_ref.at[slot, :, within, at],
                                out_ref.at[lane],
                                sems.at[spot * planes + distance],
                            )
                        )
                else:
                    copies.append(
                        pltpu.make_async_copy(
                            table_ref.at[slot, :, within], slab_ref.at[spot], sems.at[spot]
                        )
                    )
            for copy in copies:
                copy.start()
            for copy in copies:
                copy.wait()
            if not direct:
                for spot, outs in enumerate((leaving, staying)):
                    for target in range(planes):
                        piece = slab_ref[spot, :, :, target * columns : (target + 1) * columns]
                        for distance, out_ref in enumerate(outs):

                            def store(out_ref=out_ref, piece=piece):
                                out_ref[lane] = piece

                            pl.when(lax.rem(plane + distance, planes) == target)(store)

        def blank():
            for out_ref in refs[: 2 * planes]:
                out_ref[lane] = jnp.zeros(out_ref.shape[1:], out_ref.dtype)

        pl.when(owned)(bring)
        pl.when(jnp.logical_not(owned))(blank)


def screen_lanes(table, table_entry, lanes, planes):
    span, points = table.shape[2:]
    rows, columns = span // PAIR, points // planes
    shape = jax.ShapeDtypeStruct((lanes, 2, rows, columns), table.dtype)
    vmem = pl.BlockSpec(memory_space=pltpu.VMEM)
    slab = (2, 2, rows, points) if columns % 128 else (1, 1, 16, 128)
    pieces = pl.pallas_call(
        functools.partial(cut_slabs, lanes, planes),
        out_shape=(shape,) * (2 * planes),
        in_specs=[
            pl.BlockSpec(memory_space=pltpu.SMEM),
            pl.BlockSpec(memory_space=pl.ANY),
        ],
        out_specs=(vmem,) * (2 * planes),
        scratch_shapes=[
            pltpu.VMEM(slab, table.dtype),
            pltpu.SemaphoreType.DMA((2 * planes,)),
        ],
        compiler_params=pltpu.CompilerParams(vmem_limit_bytes=32 << 20),
    )(table_entry, table)
    return pieces[:planes], pieces[planes:]


def compute(sizes, entry_ref, inplane_ref, depth_ref, cond_ref, *refs):
    plane_size, depth_size, slots, pieces = sizes
    planes = plane_size // PAIR
    depths = depth_size // PAIR
    spread = 2
    gathered_refs = refs[: pieces * spread]
    block_refs = refs[pieces * spread : pieces * spread + planes]
    out_ref, wide_ref, left_ref, screened_ref, half_ref, *kept_refs = refs[
        pieces * spread + planes :
    ]
    count, _, width = out_ref.shape
    columns, rows = wide_ref.shape[2:]
    group = cond_ref.shape[1]
    conduction = group // 2
    vectors = width // group
    span = vectors * rows
    for piece, kept_ref in enumerate(kept_refs):
        for spot in range(spread):
            at = pl.ds(spot * (count // spread), count // spread)
            kept_ref[at] = gathered_refs[piece * spread + spot][...]

    def valence_of(k):
        return kept_refs[0][k, : 2 * NV]

    def trial_of(k):
        if pieces > 1:
            return kept_refs[1][k]
        parts = [kept_refs[0][k, 2 * NV :, at : at + width] for at in range(0, columns, width)]
        return jnp.concatenate(parts, axis=0)

    mine = lax.axis_index("kp")
    mine_depth = lax.axis_index("kz")
    place = (lax.div(mine, PAIR), lax.rem(mine, PAIR))
    place += (lax.div(mine_depth, PAIR), lax.rem(mine_depth, PAIR))

    def point_of(spot):
        plane = lax.rem(place[0] - lax.rem(spot, planes) + planes, planes)
        rest = lax.div(spot, planes)
        depth = lax.rem(place[2] - lax.rem(rest, depths) + depths, depths)
        rest = lax.div(rest, depths)
        side = lax.rem(place[1] + lax.rem(rest, PAIR), PAIR)
        core = lax.rem(place[3] + lax.div(rest, PAIR), PAIR)
        return plane * PAIR + side, depth * PAIR + core

    def spot_of(inplane, depth_core):
        plane = lax.rem(place[0] - lax.div(inplane, PAIR) + planes, planes)
        side = lax.rem(place[1] + lax.rem(inplane, PAIR), PAIR)
        depth = lax.rem(place[2] - lax.div(depth_core, PAIR) + depths, depths)
        core = lax.rem(place[3] + lax.rem(depth_core, PAIR), PAIR)
        return ((core * PAIR + side) * depths + depth) * planes + plane

    lane = lax.broadcasted_iota(jnp.int32, (NV, width), 1)
    low = lane % group < conduction
    vector_of = lane // group
    moves = [
        (
            lax.rem(lax.rem(inplane_ref[t], plane_size) + plane_size, plane_size),
            lax.rem(lax.rem(depth_ref[t], depth_size) + depth_size, depth_size),
        )
        for t in range(2)
    ]

    def own_of(point, t):
        inplane = lax.rem(point[0] + plane_size - moves[t][0], plane_size)
        depth = lax.rem(point[1] + depth_size - moves[t][1], depth_size)
        return spot_of(inplane, depth)

    def cond_of(k):
        inplane, depth = point_of(k)
        return cond_ref[inplane * depth_size + depth]

    def exchanged(x):
        return jnp.where(
            low, pltpu.roll(x, width - conduction, 1), pltpu.roll(x, conduction, 1)
        )

    def amplitude(k, spot):
        trial = trial_of(k).astype(F32)
        cross = exchanged(trial)
        trial = jnp.where(low, trial, -trial)
        coeffs = []
        for n in range(vectors):
            a = trial if n == 0 else pltpu.roll(trial, width - n * group, 1)
            b = cross if n == 0 else pltpu.roll(cross, width - n * group, 1)
            coeffs += [a, b, b, -a]
        coeffs = jnp.concatenate(coeffs, axis=0)[:, :group].astype(BF16)
        left_ref[spot] = jnp.dot(coeffs, cond_of(k), preferred_element_type=F32).astype(BF16)

    def expand(partner, spot):
        left = left_ref[spot]
        left = jnp.concatenate(
            [left[2 * NV * i : 2 * NV * (i + 1)] for i in range(2 * vectors)], axis=1
        )
        expanded = lax.dot_general(
            valence_of(partner), left, (((0,), (0,)), ((), ())), preferred_element_type=F32
        )
        point = point_of(partner)
        for t in range(2):
            own = own_of(point, t)
            w_real = wide_ref[t, 0]
            w_imag = wide_ref[t, 1]
            for n in range(vectors):
                real = expanded[:, 2 * n * rows : (2 * n + 1) * rows]
                imag = expanded[:, (2 * n + 1) * rows : (2 * n + 2) * rows]
                at = pl.ds((t * vectors + n) * rows, rows)
                screened_ref[own, :columns, at] = (w_real * real - w_imag * imag).astype(BF16)
                screened_ref[own, columns:, at] = (w_real * imag + w_imag * real).astype(BF16)

    def halve(k, spot):
        valence = valence_of(k)
        cross = jnp.concatenate([-valence[NV:], valence[:NV]], axis=0)
        both = jnp.dot(
            jnp.concatenate([valence, cross], axis=1), screened_ref[k], preferred_element_type=F32
        )
        half_ref[spot] = (both[:, :span] + both[:, span:]).astype(BF16)

    def finish(k, spot):
        half = half_ref[spot]
        cond = cond_of(k)
        cond = jnp.concatenate([cond] * vectors, axis=0)
        image = jnp.zeros((NV, width), F32)
        for n in range(vectors):
            product = lax.dot_general(
                half[:, n * rows : (n + 1) * rows],
                cond,
                (((1,), (1,)), ((), ())),
                preferred_element_type=F32,
            )
            real = product[:NV]
            imag = product[NV:]
            term = exchanged(imag) + jnp.where(low, real, -real)
            image = jnp.where(vector_of == n, term, image)
        inplane, depth = point_of(k)
        out_ref[inplane * depth_size + depth] = image.astype(BF16)

    def in_groups(*steps):
        size = left_ref.shape[0]

        def group_of(index, carry):
            for step in steps:
                for spot in range(size):
                    step(index * size + spot, spot)
            return carry

        lax.fori_loop(0, count // size, group_of, 0)

    def widen(t, block_ref):
        for part in range(2):
            wide_ref[t, part] = block_ref[t % block_ref.shape[0], part].astype(F32).T

    for t in range(2):
        source = lax.div(entry_ref[t], PAIR * slots)
        travelled = lax.rem(place[0] - source + planes, planes)
        for distance in range(planes):
            pl.when(travelled == distance)(functools.partial(widen, t, block_refs[distance]))
    in_groups(amplitude, expand)
    in_groups(halve, finish)


def shards(orbitals, trial_vectors, screened_table, shift_inplane, shift_depth, table_entry):
    plane_size = lax.axis_size("kp")
    depth_size = lax.axis_size("kz")
    planes = plane_size // PAIR
    depths = depth_size // PAIR
    count = plane_size * depth_size
    vectors = trial_vectors.shape[2]
    conduction = orbitals.shape[3] - NV
    points = orbitals.shape[4]
    width = vectors * 2 * conduction
    axes = ("kp", "kz")
    slots = screened_table.shape[0]

    def run(lanes):
        leaving, staying = screen_lanes(screened_table, table_entry, lanes, planes)
        leaving, own_orbitals, own_trial = lax.optimization_barrier(
            (leaving, orbitals[0, 0], trial_vectors[0, 0])
        )
        order = list(range(1, planes)) + [0]
        blocks = [None] * planes
        for distance in order:
            blocks[distance] = staying[distance] + swapped(leaving[distance], "kp")
        cond, parts = packed(own_orbitals, own_trial, planes, depths)
        parts = [collected(part) for part in parts]
        blocks = tuple(
            passed_along(block, distance) if distance else block
            for distance, block in enumerate(blocks)
        )
        blocks = list(blocks)
        cond, parts, blocks[1] = lax.optimization_barrier((cond, parts, blocks[1]))
        cond = lax.all_to_all(cond, axes, 0, 0, tiled=True)
        blocks = tuple(blocks)
        parts = [jnp.concatenate(gathered(part, depths)) for part in parts]
        parts = [[part, swapped(part, "kz")] for part in parts]
        rows, columns = blocks[0].shape[2:]
        batch = math.gcd(count, GROUP)
        operands = (cond,) + sum(map(tuple, parts), ()) + blocks
        vmem = pl.BlockSpec(memory_space=pltpu.VMEM)
        smem = pl.BlockSpec(memory_space=pltpu.SMEM)
        partial = pl.pallas_call(
            functools.partial(compute, (plane_size, depth_size, slots, len(parts))),
            out_shape=jax.ShapeDtypeStruct((count, NV, width), BF16),
            in_specs=[smem] * 3 + [vmem] * len(operands),
            out_specs=vmem,
            scratch_shapes=[
                pltpu.VMEM((2, 2, columns, rows), F32),
                pltpu.VMEM((batch, vectors * 4 * NV, rows), BF16),
                pltpu.VMEM((count, 2 * columns, 2 * vectors * rows), BF16),
                pltpu.VMEM((batch, 2 * NV, vectors * rows), BF16),
            ]
            + [pltpu.VMEM((count,) + part[0].shape[1:], BF16) for part in parts],
            compiler_params=pltpu.CompilerParams(vmem_limit_bytes=60 << 20),
        )(table_entry, shift_inplane, shift_depth, *operands)
        terms = lax.all_to_all(partial, axes, 0, 0, tiled=True)
        image = jnp.sum(terms.astype(F32), axis=0)
        image = image.reshape(NV, vectors, 2, conduction).transpose(1, 2, 3, 0)
        return image.reshape(1, 1, vectors, 2, conduction * NV)

    owner_plane = lax.div(table_entry, PAIR * slots)
    return lax.cond(
        jnp.sum(owner_plane * jnp.array([1, -1], jnp.int32)) == 0,
        functools.partial(run, 2),
        functools.partial(run, 1),
    )


def solution(mesh):
    in_specs = (
        P("kp", "kz", None, None, None),
        P("kp", "kz", None, None, None),
        P("kp", None, "kz", None),
        P(),
        P(),
        P(),
    )
    out_specs = P("kp", "kz", None, None, None)
    return jax.shard_map(shards, mesh=mesh, in_specs=in_specs, out_specs=out_specs, check_vma=False)
```

```python
import functools
import math

import jax
import jax.numpy as jnp
from jax import lax
from jax.experimental import pallas as pl
from jax.experimental.pallas import tpu as pltpu
from jax.sharding import PartitionSpec as P

NV = 32
PAIR = 2
GROUP = 8
F32 = jnp.float32
BF16 = jnp.bfloat16


def swapped(block, axis):
    return lax.ppermute(block, axis, [(i, i ^ 1) for i in range(lax.axis_size(axis))])


def passed_along(block, distance):
    size = lax.axis_size("kp")
    return lax.ppermute(block, "kp", [(i, (i + PAIR * distance) % size) for i in range(size)])


def neighbour(block, flip, distance):
    planes_sides = lax.axis_size("kp")
    size = lax.axis_size("kz")
    route = []
    for p in range(planes_sides):
        for k in range(size):
            to = (p ^ flip) * size + (k + PAIR * distance) % size
            route.append((p * size + k, to))
    return lax.ppermute(block, ("kp", "kz"), route)


def merged(columns, width):
    return columns % width == 0 and NV * width % columns == 0 and NV * width // columns % 16 == 0


def cut_orbitals(planes, orbitals_ref, trial_ref, cond_ref, *bundle_refs):
    points = orbitals_ref.shape[2]
    columns = points // planes
    count, _, rows = cond_ref.shape
    blocks = points // rows
    depths = blocks // PAIR // PAIR
    plane = lax.div(lax.axis_index("kp"), PAIR)
    cond = jnp.concatenate([orbitals_ref[0, NV:], orbitals_ref[1, NV:]], axis=0)
    for block in range(blocks):
        piece = cond[:, block * rows : (block + 1) * rows]
        side, depth_core = block % PAIR, block // PAIR
        for target in range(planes):
            cond_ref[(target * PAIR + side) * depths * PAIR + depth_core] = piece
    share = bundle_refs[0].shape[0] - 2 * NV
    width = trial_ref.shape[1]

    def fill(ref, at):
        for part in range(2):
            ref[part * NV : (part + 1) * NV] = orbitals_ref[part, :NV, at]

    for distance, ref in enumerate(bundle_refs):
        target = lax.rem(plane + distance, planes)
        if columns % 128 == 0:
            fill(ref, pl.ds(pl.multiple_of(target * columns, columns), columns))
        else:
            for spot in range(planes):
                at = slice(spot * columns, (spot + 1) * columns)
                pl.when(target == spot)(functools.partial(fill, ref, at))
        if share:
            for piece in range(columns // width):
                ref[2 * NV :, piece * width : (piece + 1) * width] = trial_ref[
                    piece * share : (piece + 1) * share
                ]


def packed(orbitals, trial_vectors, planes, depths):
    bands, points = orbitals.shape[1:]
    vectors = trial_vectors.shape[0]
    conduction = bands - NV
    columns = points // planes
    rows = points // (depths * PAIR * PAIR)
    count = planes * PAIR * depths * PAIR
    width = vectors * 2 * conduction
    trial = trial_vectors.reshape(vectors, 2, conduction, NV).transpose(3, 0, 1, 2)
    trial = trial.reshape(NV, width)
    share = NV * width // columns if merged(columns, width) else 0
    cond_shape = jax.ShapeDtypeStruct((count, 2 * conduction, rows), orbitals.dtype)
    bundle_shape = jax.ShapeDtypeStruct((2 * NV + share, columns), orbitals.dtype)
    vmem = pl.BlockSpec(memory_space=pltpu.VMEM)
    cond, *bundles = pl.pallas_call(
        functools.partial(cut_orbitals, planes),
        out_shape=(cond_shape,) + (bundle_shape,) * planes,
        in_specs=[vmem, vmem],
        out_specs=(vmem,) * (planes + 1),
        compiler_params=pltpu.CompilerParams(vmem_limit_bytes=32 << 20),
    )(orbitals, trial)
    parts = [bundles]
    if not share:
        parts.append([trial] * planes)
    return cond, parts


def collected(blocks):
    return jnp.stack(
        [passed_along(block, d) if d else block for d, block in enumerate(blocks)]
    )


def gathered(column, depths):
    here = [
        neighbour(column, flip, distance) if flip or distance else column
        for flip in range(PAIR)
        for distance in range(depths)
    ]
    return here


def cut_slabs(lanes, planes, entry_ref, table_ref, *refs):
    leaving, staying = refs[:planes], refs[planes : 2 * planes]
    slab_ref, sems = refs[2 * planes :]
    slots = table_ref.shape[0]
    points = table_ref.shape[3]
    rows, columns = leaving[0].shape[2:]
    direct = columns % 128 == 0
    mine = lax.axis_index("kp")
    plane = lax.div(mine, PAIR)
    side = lax.rem(mine, PAIR)
    for lane in range(lanes):
        entry = entry_ref[lane]
        if lanes == 1:
            entry = jnp.where(lax.div(entry, slots) == mine, entry, entry_ref[1])
        slot = lax.rem(entry, slots)
        owned = lax.div(entry, slots) == mine

        def bring():
            copies = []
            for spot, (part, outs) in enumerate(((1 - side, leaving), (side, staying))):
                within = pl.ds(pl.multiple_of(part * rows, rows), rows)
                if direct:
                    for distance, out_ref in enumerate(outs):
                        start = lax.rem(plane + distance, planes) * columns
                        at = pl.ds(pl.multiple_of(start, columns), columns)
                        copies.append(
                            pltpu.make_async_copy(
                                table_ref.at[slot, :, within, at],
                                out_ref.at[lane],
                                sems.at[spot * planes + distance],
                            )
                        )
                else:
                    copies.append(
                        pltpu.make_async_copy(
                            table_ref.at[slot, :, within], slab_ref.at[spot], sems.at[spot]
                        )
                    )
            for copy in copies:
                copy.start()
            for copy in copies:
                copy.wait()
            if not direct:
                for spot, outs in enumerate((leaving, staying)):
                    for target in range(planes):
                        piece = slab_ref[spot, :, :, target * columns : (target + 1) * columns]
                        for distance, out_ref in enumerate(outs):

                            def store(out_ref=out_ref, piece=piece):
                                out_ref[lane] = piece

                            pl.when(lax.rem(plane + distance, planes) == target)(store)

        def blank():
            for out_ref in refs[: 2 * planes]:
                out_ref[lane] = jnp.zeros(out_ref.shape[1:], out_ref.dtype)

        pl.when(owned)(bring)
        pl.when(jnp.logical_not(owned))(blank)


def screen_lanes(table, table_entry, lanes, planes):
    span, points = table.shape[2:]
    rows, columns = span // PAIR, points // planes
    shape = jax.ShapeDtypeStruct((lanes, 2, rows, columns), table.dtype)
    vmem = pl.BlockSpec(memory_space=pltpu.VMEM)
    slab = (2, 2, rows, points) if columns % 128 else (1, 1, 16, 128)
    pieces = pl.pallas_call(
        functools.partial(cut_slabs, lanes, planes),
        out_shape=(shape,) * (2 * planes),
        in_specs=[
            pl.BlockSpec(memory_space=pltpu.SMEM),
            pl.BlockSpec(memory_space=pl.ANY),
        ],
        out_specs=(vmem,) * (2 * planes),
        scratch_shapes=[
            pltpu.VMEM(slab, table.dtype),
            pltpu.SemaphoreType.DMA((2 * planes,)),
        ],
        compiler_params=pltpu.CompilerParams(vmem_limit_bytes=32 << 20),
    )(table_entry, table)
    return pieces[:planes], pieces[planes:]


def compute(sizes, entry_ref, inplane_ref, depth_ref, cond_ref, *refs):
    plane_size, depth_size, slots, pieces = sizes
    planes = plane_size // PAIR
    depths = depth_size // PAIR
    spread = 2
    gathered_refs = refs[: pieces * spread]
    block_refs = refs[pieces * spread : pieces * spread + planes]
    out_ref, wide_ref, left_ref, screened_ref, half_ref, *kept_refs = refs[
        pieces * spread + planes :
    ]
    count, _, width = out_ref.shape
    columns, rows = wide_ref.shape[2:]
    group = cond_ref.shape[1]
    conduction = group // 2
    vectors = width // group
    span = vectors * rows
    for piece, kept_ref in enumerate(kept_refs):
        for spot in range(spread):
            at = pl.ds(spot * (count // spread), count // spread)
            kept_ref[at] = gathered_refs[piece * spread + spot][...]

    def valence_of(k):
        return kept_refs[0][k, : 2 * NV]

    def trial_of(k):
        if pieces > 1:
            return kept_refs[1][k]
        parts = [kept_refs[0][k, 2 * NV :, at : at + width] for at in range(0, columns, width)]
        return jnp.concatenate(parts, axis=0)

    mine = lax.axis_index("kp")
    mine_depth = lax.axis_index("kz")
    place = (lax.div(mine, PAIR), lax.rem(mine, PAIR))
    place += (lax.div(mine_depth, PAIR), lax.rem(mine_depth, PAIR))

    def parted(x, size):
        if size & (size - 1):
            return lax.div(x, size), lax.rem(x, size)
        return x >> (size.bit_length() - 1), x & (size - 1)

    def wrapped(x, size):
        return jnp.where(x >= size, x - size, x)

    def point_of(spot):
        rest, plane = parted(spot, planes)
        rest, depth = parted(rest, depths)
        core, side = parted(rest, PAIR)
        plane = wrapped(place[0] - plane + planes, planes)
        depth = wrapped(place[2] - depth + depths, depths)
        return plane * PAIR + (place[1] ^ side), depth * PAIR + (place[3] ^ core)

    def spot_of(inplane, depth_core):
        plane, side = parted(inplane, PAIR)
        depth, core = parted(depth_core, PAIR)
        plane = wrapped(place[0] - plane + planes, planes)
        depth = wrapped(place[2] - depth + depths, depths)
        return (((core ^ place[3]) * PAIR + (side ^ place[1])) * depths + depth) * planes + plane

    lane = lax.broadcasted_iota(jnp.int32, (NV, width), 1)
    low = lane % group < conduction
    vector_of = lane // group
    moves = [
        (
            lax.rem(lax.rem(inplane_ref[t], plane_size) + plane_size, plane_size),
            lax.rem(lax.rem(depth_ref[t], depth_size) + depth_size, depth_size),
        )
        for t in range(2)
    ]

    def own_of(point, t):
        inplane = wrapped(point[0] + plane_size - moves[t][0], plane_size)
        depth = wrapped(point[1] + depth_size - moves[t][1], depth_size)
        return spot_of(inplane, depth)

    def cond_of(k):
        inplane, depth = point_of(k)
        return cond_ref[inplane * depth_size + depth]

    def exchanged(x):
        return jnp.where(
            low, pltpu.roll(x, width - conduction, 1), pltpu.roll(x, conduction, 1)
        )

    def amplitude(k, spot):
        trial = trial_of(k).astype(F32)
        cross = exchanged(trial)
        trial = jnp.where(low, trial, -trial)
        coeffs = []
        for n in range(vectors):
            a = trial if n == 0 else pltpu.roll(trial, width - n * group, 1)
            b = cross if n == 0 else pltpu.roll(cross, width - n * group, 1)
            coeffs += [a, b, b, -a]
        coeffs = jnp.concatenate(coeffs, axis=0)[:, :group].astype(BF16)
        left_ref[spot] = jnp.dot(coeffs, cond_of(k), preferred_element_type=F32).astype(BF16)

    def expand(partner, spot):
        left = left_ref[spot]
        left = jnp.concatenate(
            [left[2 * NV * i : 2 * NV * (i + 1)] for i in range(2 * vectors)], axis=1
        )
        point = point_of(partner)
        step = min(64, columns)
        valence = valence_of(partner)
        turned = valence.T
        owns = [own_of(point, t) for t in range(2)]
        for n in range(vectors):
            mine_left = left[:, 2 * n * rows : 2 * (n + 1) * rows]
            for at in range(0, columns, step):
                expanded = jnp.dot(turned[at : at + step], mine_left, preferred_element_type=F32)
                real = expanded[:, :rows]
                imag = expanded[:, rows:]
                for t in range(2):
                    w_real = wide_ref[t, 0, at : at + step]
                    w_imag = wide_ref[t, 1, at : at + step]
                    to = pl.ds((t * vectors + n) * rows, rows)
                    screened_ref[owns[t], at : at + step, to] = (
                        w_real * real - w_imag * imag
                    ).astype(BF16)
                    screened_ref[owns[t], columns + at : columns + at + step, to] = (
                        w_real * imag + w_imag * real
                    ).astype(BF16)

    def halve(k, spot):
        valence = valence_of(k)
        cross = jnp.concatenate([-valence[NV:], valence[:NV]], axis=0)
        both = jnp.dot(
            jnp.concatenate([valence, cross], axis=1), screened_ref[k], preferred_element_type=F32
        )
        half_ref[spot] = (both[:, :span] + both[:, span:]).astype(BF16)

    def finish(k, spot):
        half = half_ref[spot]
        half = jnp.concatenate([half[:, n * rows : (n + 1) * rows] for n in range(vectors)], axis=0)
        cond = jnp.concatenate([cond_of(k)] * vectors, axis=0)
        product = lax.dot_general(
            half, cond, (((1,), (1,)), ((), ())), preferred_element_type=F32
        )
        real = product[:NV]
        imag = product[NV : 2 * NV]
        for n in range(1, vectors):
            real = jnp.where(vector_of == n, product[2 * n * NV : (2 * n + 1) * NV], real)
            imag = jnp.where(vector_of == n, product[(2 * n + 1) * NV : (2 * n + 2) * NV], imag)
        image = exchanged(imag) + jnp.where(low, real, -real)
        inplane, depth = point_of(k)
        out_ref[inplane * depth_size + depth] = image.astype(BF16)

    def in_groups(*steps):
        size = left_ref.shape[0]

        def group_of(index, carry):
            for step in steps:
                for spot in range(size):
                    step(index * size + spot, spot)
            return carry

        lax.fori_loop(0, count // size, group_of, 0)

    def widen(t, block_ref):
        for part in range(2):
            wide_ref[t, part] = block_ref[t % block_ref.shape[0], part].astype(F32).T

    for t in range(2):
        source = lax.div(entry_ref[t], PAIR * slots)
        travelled = lax.rem(place[0] - source + planes, planes)
        for distance in range(planes):
            pl.when(travelled == distance)(functools.partial(widen, t, block_refs[distance]))
    in_groups(amplitude, expand)
    in_groups(halve, finish)


def shards(orbitals, trial_vectors, screened_table, shift_inplane, shift_depth, table_entry):
    plane_size = lax.axis_size("kp")
    depth_size = lax.axis_size("kz")
    planes = plane_size // PAIR
    depths = depth_size // PAIR
    count = plane_size * depth_size
    vectors = trial_vectors.shape[2]
    conduction = orbitals.shape[3] - NV
    points = orbitals.shape[4]
    width = vectors * 2 * conduction
    axes = ("kp", "kz")
    slots = screened_table.shape[0]

    def run(lanes):
        leaving, staying = screen_lanes(screened_table, table_entry, lanes, planes)
        leaving, own_orbitals, own_trial = lax.optimization_barrier(
            (leaving, orbitals[0, 0], trial_vectors[0, 0])
        )
        order = list(range(1, planes)) + [0]
        blocks = [None] * planes
        for distance in order:
            blocks[distance] = staying[distance] + swapped(leaving[distance], "kp")
        cond, parts = packed(own_orbitals, own_trial, planes, depths)
        parts = [collected(part) for part in parts]
        if lanes == 1:
            blocks[1] = passed_along(blocks[1], 1)
        cond, parts, blocks[1] = lax.optimization_barrier((cond, parts, blocks[1]))
        cond = lax.all_to_all(cond, axes, 0, 0, tiled=True)
        for distance in range(2 if lanes == 1 else 1, planes):
            blocks[distance] = passed_along(blocks[distance], distance)
        blocks = tuple(blocks)
        parts = [jnp.concatenate(gathered(part, depths)) for part in parts]
        parts = [[part, swapped(part, "kz")] for part in parts]
        rows, columns = blocks[0].shape[2:]
        batch = math.gcd(count, GROUP)
        operands = (cond,) + sum(map(tuple, parts), ()) + blocks
        vmem = pl.BlockSpec(memory_space=pltpu.VMEM)
        smem = pl.BlockSpec(memory_space=pltpu.SMEM)
        partial = pl.pallas_call(
            functools.partial(compute, (plane_size, depth_size, slots, len(parts))),
            out_shape=jax.ShapeDtypeStruct((count, NV, width), BF16),
            in_specs=[smem] * 3 + [vmem] * len(operands),
            out_specs=vmem,
            scratch_shapes=[
                pltpu.VMEM((2, 2, columns, rows), F32),
                pltpu.VMEM((batch, vectors * 4 * NV, rows), BF16),
                pltpu.VMEM((count, 2 * columns, 2 * vectors * rows), BF16),
                pltpu.VMEM((batch, 2 * NV, vectors * rows), BF16),
            ]
            + [pltpu.VMEM((count,) + part[0].shape[1:], BF16) for part in parts],
            compiler_params=pltpu.CompilerParams(vmem_limit_bytes=60 << 20),
        )(table_entry, shift_inplane, shift_depth, *operands)
        terms = lax.all_to_all(partial, axes, 0, 0, tiled=True)
        image = jnp.sum(terms.astype(F32), axis=0)
        image = image.reshape(NV, vectors, 2, conduction).transpose(1, 2, 3, 0)
        return image.reshape(1, 1, vectors, 2, conduction * NV)

    owner_plane = lax.div(table_entry, PAIR * slots)
    return lax.cond(
        jnp.sum(owner_plane * jnp.array([1, -1], jnp.int32)) == 0,
        functools.partial(run, 2),
        functools.partial(run, 1),
    )


def solution(mesh):
    in_specs = (
        P("kp", "kz", None, None, None),
        P("kp", "kz", None, None, None),
        P("kp", None, "kz", None),
        P(),
        P(),
        P(),
    )
    out_specs = P("kp", "kz", None, None, None)
    return jax.shard_map(shards, mesh=mesh, in_specs=in_specs, out_specs=out_specs, check_vma=False)
```

```python
import functools
import math

import jax
import jax.numpy as jnp
from jax import lax
from jax.experimental import pallas as pl
from jax.experimental.pallas import tpu as pltpu
from jax.sharding import PartitionSpec as P

NV = 32
PAIR = 2
GROUP = 16
F32 = jnp.float32
BF16 = jnp.bfloat16


def swapped(block, axis):
    return lax.ppermute(block, axis, [(i, i ^ 1) for i in range(lax.axis_size(axis))])


def passed_along(block, distance):
    size = lax.axis_size("kp")
    return lax.ppermute(block, "kp", [(i, (i + PAIR * distance) % size) for i in range(size)])


def neighbour(block, flip, distance):
    planes_sides = lax.axis_size("kp")
    size = lax.axis_size("kz")
    route = []
    for p in range(planes_sides):
        for k in range(size):
            to = (p ^ flip) * size + (k + PAIR * distance) % size
            route.append((p * size + k, to))
    return lax.ppermute(block, ("kp", "kz"), route)


def merged(columns, width):
    return columns % width == 0 and NV * width % columns == 0 and NV * width // columns % 16 == 0


def cut_orbitals(planes, orbitals_ref, trial_ref, cond_ref, *bundle_refs):
    points = orbitals_ref.shape[2]
    columns = points // planes
    count, _, rows = cond_ref.shape
    blocks = points // rows
    depths = blocks // PAIR // PAIR
    plane = lax.div(lax.axis_index("kp"), PAIR)
    cond = jnp.concatenate([orbitals_ref[0, NV:], orbitals_ref[1, NV:]], axis=0)
    for block in range(blocks):
        piece = cond[:, block * rows : (block + 1) * rows]
        side, depth_core = block % PAIR, block // PAIR
        for target in range(planes):
            cond_ref[(target * PAIR + side) * depths * PAIR + depth_core] = piece
    share = bundle_refs[0].shape[0] - 2 * NV
    width = trial_ref.shape[1]

    def fill(ref, at):
        for part in range(2):
            ref[part * NV : (part + 1) * NV] = orbitals_ref[part, :NV, at]

    for distance, ref in enumerate(bundle_refs):
        target = lax.rem(plane + distance, planes)
        if columns % 128 == 0:
            fill(ref, pl.ds(pl.multiple_of(target * columns, columns), columns))
        else:
            for spot in range(planes):
                at = slice(spot * columns, (spot + 1) * columns)
                pl.when(target == spot)(functools.partial(fill, ref, at))
        if share:
            for piece in range(columns // width):
                ref[2 * NV :, piece * width : (piece + 1) * width] = trial_ref[
                    piece * share : (piece + 1) * share
                ]


def packed(orbitals, trial_vectors, planes, depths):
    bands, points = orbitals.shape[1:]
    vectors = trial_vectors.shape[0]
    conduction = bands - NV
    columns = points // planes
    rows = points // (depths * PAIR * PAIR)
    count = planes * PAIR * depths * PAIR
    width = vectors * 2 * conduction
    trial = trial_vectors.reshape(vectors, 2, conduction, NV).transpose(3, 0, 1, 2)
    trial = trial.reshape(NV, width)
    share = NV * width // columns if merged(columns, width) else 0
    cond_shape = jax.ShapeDtypeStruct((count, 2 * conduction, rows), orbitals.dtype)
    bundle_shape = jax.ShapeDtypeStruct((2 * NV + share, columns), orbitals.dtype)
    vmem = pl.BlockSpec(memory_space=pltpu.VMEM)
    cond, *bundles = pl.pallas_call(
        functools.partial(cut_orbitals, planes),
        out_shape=(cond_shape,) + (bundle_shape,) * planes,
        in_specs=[vmem, vmem],
        out_specs=(vmem,) * (planes + 1),
        compiler_params=pltpu.CompilerParams(vmem_limit_bytes=32 << 20),
    )(orbitals, trial)
    parts = [bundles]
    if not share:
        parts.append([trial] * planes)
    return cond, parts


def collected(blocks):
    return jnp.stack(
        [passed_along(block, d) if d else block for d, block in enumerate(blocks)]
    )


def gathered(column, depths):
    here = [
        neighbour(column, flip, distance) if flip or distance else column
        for flip in range(PAIR)
        for distance in range(depths)
    ]
    return here


def cut_slabs(lanes, planes, distances, entry_ref, table_ref, *refs):
    number = len(distances)
    leaving, staying = refs[:number], refs[number : 2 * number]
    slab_ref, sems = refs[2 * number :]
    slots = table_ref.shape[0]
    points = table_ref.shape[3]
    rows, columns = leaving[0].shape[2:]
    direct = columns % 128 == 0
    mine = lax.axis_index("kp")
    plane = lax.div(mine, PAIR)
    side = lax.rem(mine, PAIR)
    for lane in range(lanes):
        entry = entry_ref[lane]
        if lanes == 1:
            entry = jnp.where(lax.div(entry, slots) == mine, entry, entry_ref[1])
        slot = lax.rem(entry, slots)
        owned = lax.div(entry, slots) == mine

        def bring():
            copies = []
            for spot, (part, outs) in enumerate(((1 - side, leaving), (side, staying))):
                within = pl.ds(pl.multiple_of(part * rows, rows), rows)
                if direct:
                    for place, (distance, out_ref) in enumerate(zip(distances, outs)):
                        start = lax.rem(plane + distance, planes) * columns
                        at = pl.ds(pl.multiple_of(start, columns), columns)
                        copies.append(
                            pltpu.make_async_copy(
                                table_ref.at[slot, :, within, at],
                                out_ref.at[lane],
                                sems.at[spot * number + place],
                            )
                        )
                else:
                    copies.append(
                        pltpu.make_async_copy(
                            table_ref.at[slot, :, within], slab_ref.at[spot], sems.at[spot]
                        )
                    )
            for copy in copies:
                copy.start()
            for copy in copies:
                copy.wait()
            if not direct:
                for spot, outs in enumerate((leaving, staying)):
                    for target in range(planes):
                        piece = slab_ref[spot, :, :, target * columns : (target + 1) * columns]
                        for distance, out_ref in zip(distances, outs):

                            def store(out_ref=out_ref, piece=piece):
                                out_ref[lane] = piece

                            pl.when(lax.rem(plane + distance, planes) == target)(store)

        def blank():
            for out_ref in refs[: 2 * number]:
                out_ref[lane] = jnp.zeros(out_ref.shape[1:], out_ref.dtype)

        pl.when(owned)(bring)
        pl.when(jnp.logical_not(owned))(blank)


def screen_lanes(table, table_entry, lanes, planes, distances):
    span, points = table.shape[2:]
    rows, columns = span // PAIR, points // planes
    shape = jax.ShapeDtypeStruct((lanes, 2, rows, columns), table.dtype)
    vmem = pl.BlockSpec(memory_space=pltpu.VMEM)
    slab = (2, 2, rows, points) if columns % 128 else (1, 1, 16, 128)
    number = len(distances)
    pieces = pl.pallas_call(
        functools.partial(cut_slabs, lanes, planes, distances),
        out_shape=(shape,) * (2 * number),
        in_specs=[
            pl.BlockSpec(memory_space=pltpu.SMEM),
            pl.BlockSpec(memory_space=pl.ANY),
        ],
        out_specs=(vmem,) * (2 * number),
        scratch_shapes=[
            pltpu.VMEM(slab, table.dtype),
            pltpu.SemaphoreType.DMA((2 * number,)),
        ],
        compiler_params=pltpu.CompilerParams(vmem_limit_bytes=32 << 20),
    )(table_entry, table)
    return pieces[:number], pieces[number:]


def compute(sizes, entry_ref, inplane_ref, depth_ref, cond_ref, *refs):
    plane_size, depth_size, slots, pieces = sizes
    planes = plane_size // PAIR
    depths = depth_size // PAIR
    spread = 2
    gathered_refs = refs[: pieces * spread]
    block_refs = refs[pieces * spread : pieces * spread + planes]
    out_ref, wide_ref, left_ref, screened_ref, half_ref, *kept_refs = refs[
        pieces * spread + planes :
    ]
    count, _, width = out_ref.shape
    columns, rows = wide_ref.shape[2:]
    group = cond_ref.shape[1]
    conduction = group // 2
    vectors = width // group
    span = vectors * rows
    for piece, kept_ref in enumerate(kept_refs):
        for spot in range(spread):
            at = pl.ds(spot * (count // spread), count // spread)
            kept_ref[at] = gathered_refs[piece * spread + spot][...]

    def valence_of(k):
        return kept_refs[0][k, : 2 * NV]

    def trial_of(k):
        if pieces > 1:
            return kept_refs[1][k]
        parts = [kept_refs[0][k, 2 * NV :, at : at + width] for at in range(0, columns, width)]
        return jnp.concatenate(parts, axis=0)

    mine = lax.axis_index("kp")
    mine_depth = lax.axis_index("kz")
    place = (lax.div(mine, PAIR), lax.rem(mine, PAIR))
    place += (lax.div(mine_depth, PAIR), lax.rem(mine_depth, PAIR))

    def parted(x, size):
        if size & (size - 1):
            return lax.div(x, size), lax.rem(x, size)
        return x >> (size.bit_length() - 1), x & (size - 1)

    def wrapped(x, size):
        return jnp.where(x >= size, x - size, x)

    def point_of(spot):
        rest, plane = parted(spot, planes)
        rest, depth = parted(rest, depths)
        core, side = parted(rest, PAIR)
        plane = wrapped(place[0] - plane + planes, planes)
        depth = wrapped(place[2] - depth + depths, depths)
        return plane * PAIR + (place[1] ^ side), depth * PAIR + (place[3] ^ core)

    def spot_of(inplane, depth_core):
        plane, side = parted(inplane, PAIR)
        depth, core = parted(depth_core, PAIR)
        plane = wrapped(place[0] - plane + planes, planes)
        depth = wrapped(place[2] - depth + depths, depths)
        return (((core ^ place[3]) * PAIR + (side ^ place[1])) * depths + depth) * planes + plane

    lane = lax.broadcasted_iota(jnp.int32, (NV, width), 1)
    low = lane % group < conduction
    vector_of = lane // group
    moves = [
        (
            lax.rem(lax.rem(inplane_ref[t], plane_size) + plane_size, plane_size),
            lax.rem(lax.rem(depth_ref[t], depth_size) + depth_size, depth_size),
        )
        for t in range(2)
    ]

    def own_of(point, t):
        inplane = wrapped(point[0] + plane_size - moves[t][0], plane_size)
        depth = wrapped(point[1] + depth_size - moves[t][1], depth_size)
        return spot_of(inplane, depth)

    def cond_of(k):
        inplane, depth = point_of(k)
        return cond_ref[inplane * depth_size + depth]

    def exchanged(x):
        return jnp.where(
            low, pltpu.roll(x, width - conduction, 1), pltpu.roll(x, conduction, 1)
        )

    def amplitude(k, spot):
        trial = trial_of(k).astype(F32)
        cross = exchanged(trial)
        trial = jnp.where(low, trial, -trial)
        coeffs = []
        for n in range(vectors):
            a = trial if n == 0 else pltpu.roll(trial, width - n * group, 1)
            b = cross if n == 0 else pltpu.roll(cross, width - n * group, 1)
            coeffs += [a, b, b, -a]
        coeffs = jnp.concatenate(coeffs, axis=0)[:, :group].astype(BF16)
        left_ref[spot] = jnp.dot(coeffs, cond_of(k), preferred_element_type=F32).astype(BF16)

    def expand(partner, spot):
        left = left_ref[spot]
        left = jnp.concatenate(
            [left[2 * NV * i : 2 * NV * (i + 1)] for i in range(2 * vectors)], axis=1
        )
        point = point_of(partner)
        step = min(64, columns)
        valence = valence_of(partner)
        turned = valence.T
        owns = [own_of(point, t) for t in range(2)]
        for n in range(vectors):
            mine_left = left[:, 2 * n * rows : 2 * (n + 1) * rows]
            for at in range(0, columns, step):
                expanded = jnp.dot(turned[at : at + step], mine_left, preferred_element_type=F32)
                real = expanded[:, :rows]
                imag = expanded[:, rows:]
                for t in range(2):
                    w_real = wide_ref[t, 0, at : at + step]
                    w_imag = wide_ref[t, 1, at : at + step]
                    to = pl.ds((t * vectors + n) * rows, rows)
                    screened_ref[owns[t], at : at + step, to] = (
                        w_real * real - w_imag * imag
                    ).astype(BF16)
                    screened_ref[owns[t], columns + at : columns + at + step, to] = (
                        w_real * imag + w_imag * real
                    ).astype(BF16)

    def halve(k, spot):
        valence = valence_of(k)
        cross = jnp.concatenate([-valence[NV:], valence[:NV]], axis=0)
        both = jnp.dot(
            jnp.concatenate([valence, cross], axis=1), screened_ref[k], preferred_element_type=F32
        )
        half_ref[spot] = (both[:, :span] + both[:, span:]).astype(BF16)

    def finish(k, spot):
        half = half_ref[spot]
        half = jnp.concatenate([half[:, n * rows : (n + 1) * rows] for n in range(vectors)], axis=0)
        cond = jnp.concatenate([cond_of(k)] * vectors, axis=0)
        product = lax.dot_general(
            half, cond, (((1,), (1,)), ((), ())), preferred_element_type=F32
        )
        real = product[:NV]
        imag = product[NV : 2 * NV]
        for n in range(1, vectors):
            real = jnp.where(vector_of == n, product[2 * n * NV : (2 * n + 1) * NV], real)
            imag = jnp.where(vector_of == n, product[(2 * n + 1) * NV : (2 * n + 2) * NV], imag)
        image = exchanged(imag) + jnp.where(low, real, -real)
        inplane, depth = point_of(k)
        out_ref[inplane * depth_size + depth] = image.astype(BF16)

    def in_groups(*steps):
        size = left_ref.shape[0]

        def group_of(index, carry):
            for step in steps:
                for spot in range(size):
                    step(index * size + spot, spot)
            return carry

        lax.fori_loop(0, count // size, group_of, 0)

    def widen(t, block_ref):
        for part in range(2):
            wide_ref[t, part] = block_ref[t % block_ref.shape[0], part].astype(F32).T

    for t in range(2):
        source = lax.div(entry_ref[t], PAIR * slots)
        travelled = lax.rem(place[0] - source + planes, planes)
        for distance in range(planes):
            pl.when(travelled == distance)(functools.partial(widen, t, block_refs[distance]))
    in_groups(amplitude, expand)
    in_groups(halve, finish)


def shards(orbitals, trial_vectors, screened_table, shift_inplane, shift_depth, table_entry):
    plane_size = lax.axis_size("kp")
    depth_size = lax.axis_size("kz")
    planes = plane_size // PAIR
    depths = depth_size // PAIR
    count = plane_size * depth_size
    vectors = trial_vectors.shape[2]
    conduction = orbitals.shape[3] - NV
    points = orbitals.shape[4]
    width = vectors * 2 * conduction
    axes = ("kp", "kz")
    slots = screened_table.shape[0]

    def run(lanes):
        blocks = [None] * planes
        own_orbitals, own_trial = orbitals[0, 0], trial_vectors[0, 0]
        for distances in ([1], list(range(2, planes)) + [0]):
            leaving, staying = screen_lanes(screened_table, table_entry, lanes, planes, distances)
            if distances[0] == 1:
                leaving, own_orbitals, own_trial = lax.optimization_barrier(
                    (leaving, own_orbitals, own_trial)
                )
            for spot, distance in enumerate(distances):
                blocks[distance] = staying[spot] + swapped(leaving[spot], "kp")
        cond, parts = packed(own_orbitals, own_trial, planes, depths)
        parts = [collected(part) for part in parts]
        if lanes == 1:
            blocks[1] = passed_along(blocks[1], 1)
        cond, parts, blocks[1] = lax.optimization_barrier((cond, parts, blocks[1]))
        cond = lax.all_to_all(cond, axes, 0, 0, tiled=True)
        for distance in range(2 if lanes == 1 else 1, planes):
            blocks[distance] = passed_along(blocks[distance], distance)
        blocks = tuple(blocks)
        parts = [jnp.concatenate(gathered(part, depths)) for part in parts]
        parts = [[part, swapped(part, "kz")] for part in parts]
        rows, columns = blocks[0].shape[2:]
        batch = math.gcd(count, GROUP)
        operands = (cond,) + sum(map(tuple, parts), ()) + blocks
        vmem = pl.BlockSpec(memory_space=pltpu.VMEM)
        smem = pl.BlockSpec(memory_space=pltpu.SMEM)
        partial = pl.pallas_call(
            functools.partial(compute, (plane_size, depth_size, slots, len(parts))),
            out_shape=jax.ShapeDtypeStruct((count, NV, width), BF16),
            in_specs=[smem] * 3 + [vmem] * len(operands),
            out_specs=vmem,
            scratch_shapes=[
                pltpu.VMEM((2, 2, columns, rows), F32),
                pltpu.VMEM((batch, vectors * 4 * NV, rows), BF16),
                pltpu.VMEM((count, 2 * columns, 2 * vectors * rows), BF16),
                pltpu.VMEM((batch, 2 * NV, vectors * rows), BF16),
            ]
            + [pltpu.VMEM((count,) + part[0].shape[1:], BF16) for part in parts],
            compiler_params=pltpu.CompilerParams(vmem_limit_bytes=60 << 20),
        )(table_entry, shift_inplane, shift_depth, *operands)
        terms = lax.all_to_all(partial, axes, 0, 0, tiled=True)
        image = jnp.sum(terms.astype(F32), axis=0)
        image = image.reshape(NV, vectors, 2, conduction).transpose(1, 2, 3, 0)
        return image.reshape(1, 1, vectors, 2, conduction * NV)

    owner_plane = lax.div(table_entry, PAIR * slots)
    return lax.cond(
        jnp.sum(owner_plane * jnp.array([1, -1], jnp.int32)) == 0,
        functools.partial(run, 2),
        functools.partial(run, 1),
    )


def solution(mesh):
    in_specs = (
        P("kp", "kz", None, None, None),
        P("kp", "kz", None, None, None),
        P("kp", None, "kz", None),
        P(),
        P(),
        P(),
    )
    out_specs = P("kp", "kz", None, None, None)
    return jax.shard_map(shards, mesh=mesh, in_specs=in_specs, out_specs=out_specs, check_vma=False)
```

```python
import functools
import math

import jax
import jax.numpy as jnp
from jax import lax
from jax.experimental import pallas as pl
from jax.experimental.pallas import tpu as pltpu
from jax.sharding import PartitionSpec as P

NV = 32
PAIR = 2
GROUP = 16
F32 = jnp.float32
BF16 = jnp.bfloat16


def swapped(block, axis):
    return lax.ppermute(block, axis, [(i, i ^ 1) for i in range(lax.axis_size(axis))])


def passed_along(block, distance):
    size = lax.axis_size("kp")
    return lax.ppermute(block, "kp", [(i, (i + PAIR * distance) % size) for i in range(size)])


def neighbour(block, flip, distance):
    planes_sides = lax.axis_size("kp")
    size = lax.axis_size("kz")
    route = []
    for p in range(planes_sides):
        for k in range(size):
            to = (p ^ flip) * size + (k + PAIR * distance) % size
            route.append((p * size + k, to))
    return lax.ppermute(block, ("kp", "kz"), route)


def merged(columns, width):
    return columns % width == 0 and NV * width % columns == 0 and NV * width // columns % 16 == 0


def cut_orbitals(planes, orbitals_ref, trial_ref, cond_ref, *bundle_refs):
    points = orbitals_ref.shape[2]
    columns = points // planes
    count, _, rows = cond_ref.shape
    blocks = points // rows
    depths = blocks // PAIR // PAIR
    plane = lax.div(lax.axis_index("kp"), PAIR)
    cond = jnp.concatenate([orbitals_ref[0, NV:], orbitals_ref[1, NV:]], axis=0)
    for block in range(blocks):
        piece = cond[:, block * rows : (block + 1) * rows]
        side, depth_core = block % PAIR, block // PAIR
        for target in range(planes):
            cond_ref[(target * PAIR + side) * depths * PAIR + depth_core] = piece
    share = bundle_refs[0].shape[0] - 2 * NV
    width = trial_ref.shape[1]

    def fill(ref, at):
        for part in range(2):
            ref[part * NV : (part + 1) * NV] = orbitals_ref[part, :NV, at]

    for distance, ref in enumerate(bundle_refs):
        target = lax.rem(plane + distance, planes)
        if columns % 128 == 0:
            fill(ref, pl.ds(pl.multiple_of(target * columns, columns), columns))
        else:
            for spot in range(planes):
                at = slice(spot * columns, (spot + 1) * columns)
                pl.when(target == spot)(functools.partial(fill, ref, at))
        if share:
            for piece in range(columns // width):
                ref[2 * NV :, piece * width : (piece + 1) * width] = trial_ref[
                    piece * share : (piece + 1) * share
                ]


def packed(orbitals, trial_vectors, planes, depths):
    bands, points = orbitals.shape[1:]
    vectors = trial_vectors.shape[0]
    conduction = bands - NV
    columns = points // planes
    rows = points // (depths * PAIR * PAIR)
    count = planes * PAIR * depths * PAIR
    width = vectors * 2 * conduction
    trial = trial_vectors.reshape(vectors, 2, conduction, NV).transpose(3, 0, 1, 2)
    trial = trial.reshape(NV, width)
    share = NV * width // columns if merged(columns, width) else 0
    cond_shape = jax.ShapeDtypeStruct((count, 2 * conduction, rows), orbitals.dtype)
    bundle_shape = jax.ShapeDtypeStruct((2 * NV + share, columns), orbitals.dtype)
    vmem = pl.BlockSpec(memory_space=pltpu.VMEM)
    cond, *bundles = pl.pallas_call(
        functools.partial(cut_orbitals, planes),
        out_shape=(cond_shape,) + (bundle_shape,) * planes,
        in_specs=[vmem, vmem],
        out_specs=(vmem,) * (planes + 1),
        compiler_params=pltpu.CompilerParams(vmem_limit_bytes=32 << 20),
    )(orbitals, trial)
    parts = [bundles]
    if not share:
        parts.append([trial] * planes)
    return cond, parts


def collected(blocks):
    return jnp.stack(
        [passed_along(block, d) if d else block for d, block in enumerate(blocks)]
    )


def gathered(column, depths):
    here = [
        neighbour(column, flip, distance) if flip or distance else column
        for flip in range(PAIR)
        for distance in range(depths)
    ]
    return here


def cut_slabs(lanes, planes, distances, entry_ref, table_ref, *refs):
    number = len(distances)
    leaving, staying = refs[:number], refs[number : 2 * number]
    slab_ref, sems = refs[2 * number :]
    slots = table_ref.shape[0]
    points = table_ref.shape[3]
    rows, columns = leaving[0].shape[2:]
    direct = columns % 128 == 0
    mine = lax.axis_index("kp")
    plane = lax.div(mine, PAIR)
    side = lax.rem(mine, PAIR)
    for lane in range(lanes):
        entry = entry_ref[lane]
        if lanes == 1:
            entry = jnp.where(lax.div(entry, slots) == mine, entry, entry_ref[1])
        slot = lax.rem(entry, slots)
        owned = lax.div(entry, slots) == mine

        def bring():
            copies = []
            for spot, (part, outs) in enumerate(((1 - side, leaving), (side, staying))):
                within = pl.ds(pl.multiple_of(part * rows, rows), rows)
                if direct:
                    for place, (distance, out_ref) in enumerate(zip(distances, outs)):
                        start = lax.rem(plane + distance, planes) * columns
                        at = pl.ds(pl.multiple_of(start, columns), columns)
                        copies.append(
                            pltpu.make_async_copy(
                                table_ref.at[slot, :, within, at],
                                out_ref.at[lane],
                                sems.at[spot * number + place],
                            )
                        )
                else:
                    copies.append(
                        pltpu.make_async_copy(
                            table_ref.at[slot, :, within], slab_ref.at[spot], sems.at[spot]
                        )
                    )
            for copy in copies:
                copy.start()
            for copy in copies:
                copy.wait()
            if not direct:
                for spot, outs in enumerate((leaving, staying)):
                    for target in range(planes):
                        piece = slab_ref[spot, :, :, target * columns : (target + 1) * columns]
                        for distance, out_ref in zip(distances, outs):

                            def store(out_ref=out_ref, piece=piece):
                                out_ref[lane] = piece

                            pl.when(lax.rem(plane + distance, planes) == target)(store)

        def blank():
            for out_ref in refs[: 2 * number]:
                out_ref[lane] = jnp.zeros(out_ref.shape[1:], out_ref.dtype)

        pl.when(owned)(bring)
        pl.when(jnp.logical_not(owned))(blank)


def screen_lanes(table, table_entry, lanes, planes, distances):
    span, points = table.shape[2:]
    rows, columns = span // PAIR, points // planes
    shape = jax.ShapeDtypeStruct((lanes, 2, rows, columns), table.dtype)
    vmem = pl.BlockSpec(memory_space=pltpu.VMEM)
    slab = (2, 2, rows, points) if columns % 128 else (1, 1, 16, 128)
    number = len(distances)
    pieces = pl.pallas_call(
        functools.partial(cut_slabs, lanes, planes, distances),
        out_shape=(shape,) * (2 * number),
        in_specs=[
            pl.BlockSpec(memory_space=pltpu.SMEM),
            pl.BlockSpec(memory_space=pl.ANY),
        ],
        out_specs=(vmem,) * (2 * number),
        scratch_shapes=[
            pltpu.VMEM(slab, table.dtype),
            pltpu.SemaphoreType.DMA((2 * number,)),
        ],
        compiler_params=pltpu.CompilerParams(vmem_limit_bytes=32 << 20),
    )(table_entry, table)
    return pieces[:number], pieces[number:]


def compute(sizes, entry_ref, inplane_ref, depth_ref, cond_ref, *refs):
    plane_size, depth_size, slots, pieces = sizes
    planes = plane_size // PAIR
    depths = depth_size // PAIR
    spread = 2
    gathered_refs = refs[: pieces * spread]
    block_refs = refs[pieces * spread : pieces * spread + planes]
    out_ref, wide_ref, left_ref, screened_ref, half_ref, *kept_refs = refs[
        pieces * spread + planes :
    ]
    count, _, width = out_ref.shape
    columns, rows = wide_ref.shape[2:]
    group = cond_ref.shape[1]
    conduction = group // 2
    vectors = width // group
    span = vectors * rows
    for piece, kept_ref in enumerate(kept_refs):
        for spot in range(spread):
            at = pl.ds(spot * (count // spread), count // spread)
            kept_ref[at] = gathered_refs[piece * spread + spot][...]

    def valence_of(k):
        return kept_refs[0][k, : 2 * NV]

    def trial_of(k):
        if pieces > 1:
            return kept_refs[1][k]
        parts = [kept_refs[0][k, 2 * NV :, at : at + width] for at in range(0, columns, width)]
        return jnp.concatenate(parts, axis=0)

    mine = lax.axis_index("kp")
    mine_depth = lax.axis_index("kz")
    place = (lax.div(mine, PAIR), lax.rem(mine, PAIR))
    place += (lax.div(mine_depth, PAIR), lax.rem(mine_depth, PAIR))

    def parted(x, size):
        if size & (size - 1):
            return lax.div(x, size), lax.rem(x, size)
        return x >> (size.bit_length() - 1), x & (size - 1)

    def wrapped(x, size):
        return jnp.where(x >= size, x - size, x)

    def point_of(spot):
        rest, plane = parted(spot, planes)
        rest, depth = parted(rest, depths)
        core, side = parted(rest, PAIR)
        plane = wrapped(place[0] - plane + planes, planes)
        depth = wrapped(place[2] - depth + depths, depths)
        return plane * PAIR + (place[1] ^ side), depth * PAIR + (place[3] ^ core)

    def spot_of(inplane, depth_core):
        plane, side = parted(inplane, PAIR)
        depth, core = parted(depth_core, PAIR)
        plane = wrapped(place[0] - plane + planes, planes)
        depth = wrapped(place[2] - depth + depths, depths)
        return (((core ^ place[3]) * PAIR + (side ^ place[1])) * depths + depth) * planes + plane

    lane = lax.broadcasted_iota(jnp.int32, (NV, width), 1)
    low = lane % group < conduction
    vector_of = lane // group
    moves = [
        (
            lax.rem(lax.rem(inplane_ref[t], plane_size) + plane_size, plane_size),
            lax.rem(lax.rem(depth_ref[t], depth_size) + depth_size, depth_size),
        )
        for t in range(2)
    ]

    def own_of(point, t):
        inplane = wrapped(point[0] + plane_size - moves[t][0], plane_size)
        depth = wrapped(point[1] + depth_size - moves[t][1], depth_size)
        return spot_of(inplane, depth)

    def cond_of(k):
        inplane, depth = point_of(k)
        return cond_ref[inplane * depth_size + depth]

    def exchanged(x):
        return jnp.where(
            low, pltpu.roll(x, width - conduction, 1), pltpu.roll(x, conduction, 1)
        )

    def amplitude(k, spot):
        trial = trial_of(k).astype(F32)
        cross = exchanged(trial)
        trial = jnp.where(low, trial, -trial)
        coeffs = []
        for n in range(vectors):
            a = trial if n == 0 else pltpu.roll(trial, width - n * group, 1)
            b = cross if n == 0 else pltpu.roll(cross, width - n * group, 1)
            coeffs += [a, b, b, -a]
        coeffs = jnp.concatenate(coeffs, axis=0)[:, :group].astype(BF16)
        left_ref[spot] = jnp.dot(coeffs, cond_of(k), preferred_element_type=F32).astype(BF16)

    def expand(partner, spot):
        left = left_ref[spot]
        left = jnp.concatenate(
            [left[2 * NV * i : 2 * NV * (i + 1)] for i in range(2 * vectors)], axis=1
        )
        point = point_of(partner)
        step = min(64, columns)
        valence = valence_of(partner)
        turned = valence.T
        owns = [own_of(point, t) for t in range(2)]
        for n in range(vectors):
            mine_left = left[:, 2 * n * rows : 2 * (n + 1) * rows]
            for at in range(0, columns, step):
                expanded = jnp.dot(turned[at : at + step], mine_left, preferred_element_type=F32)
                real = expanded[:, :rows]
                imag = expanded[:, rows:]
                for t in range(2):
                    w_real = wide_ref[t, 0, at : at + step]
                    w_imag = wide_ref[t, 1, at : at + step]
                    to = pl.ds((t * vectors + n) * rows, rows)
                    screened_ref[owns[t], at : at + step, to] = (
                        w_real * real - w_imag * imag
                    ).astype(BF16)
                    screened_ref[owns[t], columns + at : columns + at + step, to] = (
                        w_real * imag + w_imag * real
                    ).astype(BF16)

    def halve(k, spot):
        valence = valence_of(k)
        cross = jnp.concatenate([-valence[NV:], valence[:NV]], axis=0)
        both = jnp.dot(
            jnp.concatenate([valence, cross], axis=1), screened_ref[k], preferred_element_type=F32
        )
        half_ref[spot] = (both[:, :span] + both[:, span:]).astype(BF16)

    def finish(k, spot):
        half = half_ref[spot]
        half = jnp.concatenate([half[:, n * rows : (n + 1) * rows] for n in range(vectors)], axis=0)
        cond = jnp.concatenate([cond_of(k)] * vectors, axis=0)
        product = lax.dot_general(
            half, cond, (((1,), (1,)), ((), ())), preferred_element_type=F32
        )
        real = product[:NV]
        imag = product[NV : 2 * NV]
        for n in range(1, vectors):
            real = jnp.where(vector_of == n, product[2 * n * NV : (2 * n + 1) * NV], real)
            imag = jnp.where(vector_of == n, product[(2 * n + 1) * NV : (2 * n + 2) * NV], imag)
        image = exchanged(imag) + jnp.where(low, real, -real)
        inplane, depth = point_of(k)
        out_ref[inplane * depth_size + depth] = image.astype(BF16)

    def in_groups(*steps):
        size = left_ref.shape[0]

        def group_of(index, carry):
            for step in steps:
                for spot in range(size):
                    step(index * size + spot, spot)
            return carry

        lax.fori_loop(0, count // size, group_of, 0)

    def widen(t, block_ref):
        for part in range(2):
            wide_ref[t, part] = block_ref[t % block_ref.shape[0], part].astype(F32).T

    for t in range(2):
        source = lax.div(entry_ref[t], PAIR * slots)
        travelled = lax.rem(place[0] - source + planes, planes)
        for distance in range(planes):
            pl.when(travelled == distance)(functools.partial(widen, t, block_refs[distance]))
    in_groups(amplitude, expand)
    in_groups(halve, finish)


def shards(orbitals, trial_vectors, screened_table, shift_inplane, shift_depth, table_entry):
    plane_size = lax.axis_size("kp")
    depth_size = lax.axis_size("kz")
    planes = plane_size // PAIR
    depths = depth_size // PAIR
    count = plane_size * depth_size
    vectors = trial_vectors.shape[2]
    conduction = orbitals.shape[3] - NV
    points = orbitals.shape[4]
    width = vectors * 2 * conduction
    axes = ("kp", "kz")
    slots = screened_table.shape[0]

    def run(lanes):
        blocks = [None] * planes
        first = 1 if lanes == 1 else planes // 2
        others = [distance for distance in range(1, planes) if distance != first]
        own_orbitals, own_trial = orbitals[0, 0], trial_vectors[0, 0]
        for distances in ([first], others + [0]):
            leaving, staying = screen_lanes(screened_table, table_entry, lanes, planes, distances)
            if distances[0] == first:
                leaving, own_orbitals, own_trial = lax.optimization_barrier(
                    (leaving, own_orbitals, own_trial)
                )
            for spot, distance in enumerate(distances):
                blocks[distance] = staying[spot] + swapped(leaving[spot], "kp")
        cond, parts = packed(own_orbitals, own_trial, planes, depths)
        parts = [collected(part) for part in parts]
        if lanes == 1:
            blocks[first] = passed_along(blocks[first], first)
        cond, parts, blocks[first] = lax.optimization_barrier((cond, parts, blocks[first]))
        cond = lax.all_to_all(cond, axes, 0, 0, tiled=True)
        for distance in others if lanes == 1 else [first] + others:
            blocks[distance] = passed_along(blocks[distance], distance)
        blocks = tuple(blocks)
        parts = [jnp.concatenate(gathered(part, depths)) for part in parts]
        parts = [[part, swapped(part, "kz")] for part in parts]
        rows, columns = blocks[0].shape[2:]
        batch = math.gcd(count, GROUP)
        operands = (cond,) + sum(map(tuple, parts), ()) + blocks
        vmem = pl.BlockSpec(memory_space=pltpu.VMEM)
        smem = pl.BlockSpec(memory_space=pltpu.SMEM)
        partial = pl.pallas_call(
            functools.partial(compute, (plane_size, depth_size, slots, len(parts))),
            out_shape=jax.ShapeDtypeStruct((count, NV, width), BF16),
            in_specs=[smem] * 3 + [vmem] * len(operands),
            out_specs=vmem,
            scratch_shapes=[
                pltpu.VMEM((2, 2, columns, rows), F32),
                pltpu.VMEM((batch, vectors * 4 * NV, rows), BF16),
                pltpu.VMEM((count, 2 * columns, 2 * vectors * rows), BF16),
                pltpu.VMEM((batch, 2 * NV, vectors * rows), BF16),
            ]
            + [pltpu.VMEM((count,) + part[0].shape[1:], BF16) for part in parts],
            compiler_params=pltpu.CompilerParams(vmem_limit_bytes=60 << 20),
        )(table_entry, shift_inplane, shift_depth, *operands)
        terms = lax.all_to_all(partial, axes, 0, 0, tiled=True)
        image = jnp.sum(terms.astype(F32), axis=0)
        image = image.reshape(NV, vectors, 2, conduction).transpose(1, 2, 3, 0)
        return image.reshape(1, 1, vectors, 2, conduction * NV)

    owner_plane = lax.div(table_entry, PAIR * slots)
    return lax.cond(
        jnp.sum(owner_plane * jnp.array([1, -1], jnp.int32)) == 0,
        functools.partial(run, 2),
        functools.partial(run, 1),
    )


def solution(mesh):
    in_specs = (
        P("kp", "kz", None, None, None),
        P("kp", "kz", None, None, None),
        P("kp", None, "kz", None),
        P(),
        P(),
        P(),
    )
    out_specs = P("kp", "kz", None, None, None)
    return jax.shard_map(shards, mesh=mesh, in_specs=in_specs, out_specs=out_specs, check_vma=False)
```
